512 devices in a mesh: rows: 32 (over y, z_lo, core), cols: 16 (over z_hi, x).
Axes of the slice: x: 4, y: 4, z: 16 (z_hi: 4, z_lo: 4; z = z_hi * 4 + z_lo), core: 2. Of those that a mesh axis runs over, the one named last changes fastest.
Arguments:
- level_input: bfloat16 [64, 512, 2048], P(None, 'rows', 'cols'), may hold values from -6 to 6
- kernel_a: bfloat16 [64, 64, 3, 3], replicated, may hold values from -0.25 to 0.25
- kernel_b: bfloat16 [128, 64, 3, 3], replicated, may hold values from -0.25 to 0.25
- kernel_c: bfloat16 [64, 128, 3, 3], replicated, may hold values from -0.1875 to 0.1875
- kernel_d: bfloat16 [64, 64, 3, 3], replicated, may hold values from -0.25 to 0.25
- cotangent: bfloat16 [64, 512, 2048], P(None, 'rows', 'cols'), may hold values from -6 to 6
Outputs:
- result_field: bfloat16 [64, 512, 2048], P(None, 'rows', 'cols')
- input_grad: bfloat16 [64, 512, 2048], P(None, 'rows', 'cols')
- grad_a: float32 [64, 64, 3, 3], replicated
- grad_b: float32 [128, 64, 3, 3], replicated
- grad_c: float32 [64, 128, 3, 3], replicated
- grad_d: float32 [64, 64, 3, 3], replicated
The draws below stay inside these ranges and needn't reach their ends.
All inputs are finite; a program needn't handle non-finite values.
Results may differ from the reference program's by a relative error of at most 0.017.
Values may be sent and summed in bfloat16 or wider, within the bound.
A program may use at most 64 MiB of HBM per device.

```python
import math
import jax
import jax.numpy as jnp
from jax import lax

C1 = 64
C2 = 128
H1 = 512
W1 = 2048
H2 = 256
W2 = 1024


def level_of(own_key, shape, split, smallest, high):
    def one(dim, blocks):
        heights = jax.random.uniform(jax.random.fold_in(jax.random.fold_in(own_key, 6), dim), (blocks,), jnp.float32, smallest / len(split), high / len(split))
        return jnp.repeat(jnp.exp(heights), shape[dim] // blocks).reshape((-1,) + (1,) * (len(shape) - dim - 1))

    factor_of = one(*split[0])
    for cut in split[1:]:
        factor_of = factor_of * one(*cut)
    return factor_of


def gaussian(stream_key, extent, scale, reach, cuts=(), held_as=jnp.bfloat16):
    values = scale * jax.random.normal(stream_key, extent, jnp.float32)
    if cuts:
        values = values * level_of(stream_key, extent, cuts, -0.22, 0.18)
    return jnp.clip(values, -reach, reach).astype(held_as)


def setup_inputs(seed: int = 0) -> dict:
    key_of = jax.random.split(jax.random.key(seed), 7)
    return {
        "level_input": gaussian(key_of[0], (C1, H1, W1), 1.0, 6.0, ((1, 32), (2, 16))),
        "kernel_a": gaussian(key_of[1], (C1, C1, 3, 3), (9 * C1) ** -0.5, 0.25),
        "kernel_b": gaussian(key_of[2], (C2, C1, 3, 3), (9 * C1) ** -0.5, 0.25),
        "kernel_c": gaussian(key_of[3], (C1, C2, 3, 3), (9 * C2) ** -0.5, 0.1875),
        "kernel_d": gaussian(key_of[4], (C1, C1, 3, 3), (9 * C1) ** -0.5, 0.25),
        "cotangent": gaussian(key_of[5], (C1, H1, W1), 1.0, 6.0, ((1, 32), (2, 16))),
    }


def conv_valid(padded, kernel):
    result = lax.conv_general_dilated(padded[None], kernel, (1, 1), 'VALID', dimension_numbers=('NCHW', 'OIHW', 'NCHW'), preferred_element_type=jnp.float32)
    return result[0]

def kernel_grad(padded, upstream):
    height = upstream.shape[1]
    width_cells = upstream.shape[2]
    tap_list = []
    for shift_y in range(3):
        tap_row = []
        for shift_x in range(3):
            window = padded[:, shift_y:shift_y + height, shift_x:shift_x + width_cells]
            tap_row.append(lax.dot_general(upstream, window, (((1, 2), (1, 2)), ((), ())), preferred_element_type=jnp.float32))
        tap_list.append(jnp.stack(tap_row, axis=-1))
    return jnp.stack(tap_list, axis=-2)

def flipped(kernel):
    return jnp.transpose(kernel[:, :, ::-1, ::-1], (1, 0, 2, 3))

def block_view(field):
    channels, height, width_cells = field.shape
    return field.astype(jnp.float32).reshape(channels, height // 2, 2, width_cells // 2, 2)

def pooled(field):
    return lax.optimization_barrier(jnp.mean(block_view(field), axis=(2, 4))).astype(jnp.bfloat16)

def block_sum(field):
    return lax.optimization_barrier(jnp.sum(block_view(field), axis=(2, 4))).astype(jnp.bfloat16)

def upsampled(field):
    return jnp.repeat(jnp.repeat(field, 2, axis=1), 2, axis=2)

def gelu_back(preact, upstream):
    return jax.vjp(jax.nn.gelu, preact)[1](upstream)[0]

def zero_pad(field):
    return jnp.pad(field, ((0, 0), (1, 1), (1, 1)))

def reference(level_input, kernel_a, kernel_b, kernel_c, kernel_d, cotangent):
    padded_in = zero_pad(level_input)
    pre_a = conv_valid(padded_in, kernel_a)
    hidden = jax.nn.gelu(pre_a).astype(jnp.bfloat16)
    coarse = pooled(hidden)
    padded_coarse = zero_pad(coarse)
    pre_b = conv_valid(padded_coarse, kernel_b)
    middle = jax.nn.gelu(pre_b).astype(jnp.bfloat16)
    padded_middle = zero_pad(middle)
    coarse_out = conv_valid(padded_middle, kernel_c).astype(jnp.bfloat16)
    joined = (hidden.astype(jnp.float32) + upsampled(coarse_out).astype(jnp.float32)).astype(jnp.bfloat16)
    padded_joined = zero_pad(joined)
    result_field = conv_valid(padded_joined, kernel_d).astype(jnp.bfloat16)
    grad_joined = conv_valid(zero_pad(cotangent), flipped(kernel_d)).astype(jnp.bfloat16)
    sum_d = kernel_grad(padded_joined, cotangent)
    grad_coarse = block_sum(grad_joined)
    sum_c = kernel_grad(padded_middle, grad_coarse)
    grad_pre_b = gelu_back(pre_b, conv_valid(zero_pad(grad_coarse), flipped(kernel_c))).astype(jnp.bfloat16)
    sum_b = kernel_grad(padded_coarse, grad_pre_b)
    grad_pooled = conv_valid(zero_pad(grad_pre_b), flipped(kernel_b)).astype(jnp.bfloat16)
    grad_hidden = grad_joined.astype(jnp.float32) + 0.25 * upsampled(grad_pooled).astype(jnp.float32)
    grad_pre_a = gelu_back(pre_a, grad_hidden).astype(jnp.bfloat16)
    input_grad = conv_valid(zero_pad(grad_pre_a), flipped(kernel_a)).astype(jnp.bfloat16)
    sum_a = kernel_grad(padded_in, grad_pre_a)
    fine_scale = 1.0 / math.sqrt(H1 * W1)
    coarse_scale = 1.0 / math.sqrt(H2 * W2)
    return (result_field, input_grad, sum_a * fine_scale, sum_b * coarse_scale, sum_c * coarse_scale, sum_d * fine_scale)
```

```python
import math

import jax
import jax.numpy as jnp
from jax import lax
from jax.experimental import pallas as pl
from jax.experimental.pallas import tpu as pltpu
from jax.sharding import PartitionSpec as P


MESH = pl.DeviceIdType.MESH


def _reduce_kernel(x_ref, out_ref, pair_out, pair_in, plane_out, plane_in, own, near_in, far, whole,
                   pair_s, pair_r, plane_s, plane_r, near_s, near_r, far_s, far_r,
                   gnear_s, gnear_r, gplane_s, gplane_r, gpair_s, gpair_r):
    rows, cols = lax.axis_index("rows"), lax.axis_index("cols")
    y, near, core = rows // 8, (rows // 2) % 4, rows % 2
    far_at, x = cols // 4, cols % 4

    def place(y_at, near_at, core_at, z_at, x_at):
        return (y_at * 8 + near_at * 2 + core_at, z_at * 4 + x_at)

    partner = place(y, near, 1 - core, far_at, x)

    def plane_peer(dy, dx):
        return place((y + dy) % 4, near, core, far_at, (x + dx) % 4)

    def near_peer(dz):
        return place(y, (near + dz) % 4, core, far_at, x)

    def far_peer(dz):
        return place(y, near, core, (far_at + dz) % 4, x)

    plane_steps = [(dy, dx) for dy in (2, 1, 3, 0) for dx in (2, 1, 3, 0)]
    barrier = pltpu.get_barrier_semaphore()
    greeted = [partner]
    greeted += [plane_peer(dy, dx) for dy, dx in plane_steps if (dy, dx) != (0, 0)]
    greeted += [near_peer(dz) for dz in (1, 2, 3)] + [far_peer(dz) for dz in (1, 2, 3)]
    for peer in greeted:
        pl.semaphore_signal(barrier, inc=1, device_id=peer, device_id_type=MESH)

    def send(src, dst, send_sem, recv_sem, peer):
        copy = pltpu.make_async_remote_copy(
            src_ref=src, dst_ref=dst, send_sem=send_sem, recv_sem=recv_sem,
            device_id=peer, device_id_type=MESH)
        copy.start()
        return copy

    theirs, mine = (1 - core) * 64, core * 64
    started = []
    for dy in (2, 1, 3, 0):
        first = ((y + dy) % 4) * 16
        pair_out[pl.ds(first, 16)] = x_ref[pl.ds(theirs + first, 16)].astype(jnp.bfloat16)
    pl.semaphore_wait(barrier, len(greeted))
    pair = {}
    for dy in (2, 1, 3, 0):
        piece = pl.ds(((y + dy) % 4) * 16, 16)
        pair[dy] = send(pair_out.at[piece], pair_in.at[piece], pair_s.at[dy], pair_r.at[dy], partner)
    plane = {}
    for dy, dx in plane_steps:
        if dx == 2:
            pair[dy].wait_recv()
        first = ((y + dy) % 4) * 16 + ((x + dx) % 4) * 4
        chunk = pl.ds(first, 4)
        both = x_ref[pl.ds(mine + first, 4)] + pair_in[chunk].astype(jnp.float32)
        if (dy, dx) == (0, 0):
            own[...] = both
        else:
            k = dy * 4 + dx
            plane_out[chunk] = both.astype(jnp.bfloat16)
            plane[k] = send(plane_out.at[chunk], plane_in.at[k], plane_s.at[k], plane_r.at[k],
                            plane_peer(dy, dx))
    total = own[...]
    for k in (4, 12, 1, 3, 8, 2, 5, 7, 13, 15, 6, 14, 9, 11, 10):
        plane[k].wait_recv()
        total = total + plane_in[k].astype(jnp.float32)
    own[...] = total
    near_copies = {}
    for dz in (2, 1, 3):
        near_copies[dz] = send(own.at[(near + dz) % 4], near_in.at[dz], near_s.at[dz],
                               near_r.at[dz], near_peer(dz))
    tile = own[near]
    for dz in (1, 3, 2):
        near_copies[dz].wait_recv()
        tile = tile + near_in[dz]
    far[far_at] = tile
    far_copies = {}
    for dz in (2, 1, 3):
        far_copies[dz] = send(far.at[far_at], far.at[far_at], far_s.at[dz], far_r.at[dz], far_peer(dz))
    for dz in (1, 3, 2):
        far_copies[dz].wait_recv()
    tile = ((far[0] + far[1]) + far[2]) + far[3]
    base = mine + y * 16 + x * 4
    whole[base + near] = tile.astype(jnp.bfloat16)
    gather = []
    for dz in (2, 1, 3):
        at = whole.at[base + near]
        gather.append(send(at, at, gnear_s.at[dz], gnear_r.at[dz], near_peer(dz)))
    for copy in gather:
        copy.wait_recv()
    gplane = {}
    for dy, dx in plane_steps:
        if (dy, dx) != (0, 0):
            k = dy * 4 + dx
            at = whole.at[pl.ds(base, 4)]
            gplane[k] = send(at, at, gplane_s.at[k], gplane_r.at[k], plane_peer(dy, dx))
    gpair = []
    for dy in (0, 1, 3, 2):
        for dx in (0, 1, 3, 2):
            if (dy, dx) != (0, 0):
                gplane[dy * 4 + dx].wait_recv()
        at = whole.at[pl.ds(mine + ((y - dy + 4) % 4) * 16, 16)]
        gpair.append(send(at, at, gpair_s.at[dy], gpair_r.at[dy], partner))
    for copy in gpair:
        copy.wait_recv()
    out_ref[...] = whole[...].astype(jnp.float32)
    for copies in (pair.values(), plane.values(), near_copies.values(), far_copies.values(), gather,
                   gplane.values(), gpair):
        for copy in copies:
            copy.wait_send()


def reduce_all(tiles):
    dma = pltpu.SemaphoreType.DMA
    return pl.pallas_call(
        _reduce_kernel,
        out_shape=jax.ShapeDtypeStruct((128, 16, 128), jnp.float32),
        in_specs=[pl.BlockSpec(memory_space=pltpu.VMEM)],
        out_specs=pl.BlockSpec(memory_space=pltpu.VMEM),
        scratch_shapes=[
            pltpu.VMEM((64, 16, 128), jnp.bfloat16),
            pltpu.VMEM((64, 16, 128), jnp.bfloat16),
            pltpu.VMEM((64, 16, 128), jnp.bfloat16),
            pltpu.VMEM((16, 4, 16, 128), jnp.bfloat16),
            pltpu.VMEM((4, 16, 128), jnp.float32),
            pltpu.VMEM((4, 16, 128), jnp.float32),
            pltpu.VMEM((4, 16, 128), jnp.float32),
            pltpu.VMEM((128, 16, 128), jnp.bfloat16),
            dma((4,)), dma((4,)), dma((16,)), dma((16,)), dma((4,)), dma((4,)), dma((4,)), dma((4,)),
            dma((4,)), dma((4,)), dma((16,)), dma((16,)), dma((4,)), dma((4,)),
        ],
        compiler_params=pltpu.CompilerParams(
            collective_id=1, has_side_effects=True, vmem_limit_bytes=32 * 1024 * 1024),
        cost_estimate=pl.CostEstimate(flops=1000000, bytes_accessed=4000000, transcendentals=0),
    )(tiles)


def with_halo(array, sides, width):
    for axis, dim in sides:
        peers, length = (lax.axis_size(axis), array.shape[dim])
        up = [(i, (i + 1) % peers) for i in range(peers - 1)]
        down = [(j, i) for i, j in up]
        last = lax.slice_in_dim(array, length - width, length, axis=dim)
        initial = lax.slice_in_dim(array, 0, width, axis=dim)
        before = lax.ppermute(last, axis, up)
        after = lax.ppermute(initial, axis, down)
        array = jnp.concatenate([before, array, after], axis=dim)
    return array


def conv_valid(padded, kernel):
    result = lax.conv_general_dilated(
        padded[None],
        kernel,
        (1, 1),
        "VALID",
        dimension_numbers=("NCHW", "OIHW", "NCHW"),
        preferred_element_type=jnp.float32,
    )
    return result[0]


def kernel_grad(padded, upstream):
    height = upstream.shape[1]
    width_cells = upstream.shape[2]
    tap_list = []
    for shift_y in range(3):
        tap_row = []
        for shift_x in range(3):
            window = padded[:, shift_y : shift_y + height, shift_x : shift_x + width_cells]
            tap_row.append(
                lax.dot_general(
                    upstream,
                    window,
                    (((1, 2), (1, 2)), ((), ())),
                    preferred_element_type=jnp.float32,
                )
            )
        tap_list.append(jnp.stack(tap_row, axis=-1))
    return jnp.stack(tap_list, axis=-2)


def flipped(kernel):
    return jnp.transpose(kernel[:, :, ::-1, ::-1], (1, 0, 2, 3))


def block_view(field):
    channels, height, width_cells = field.shape
    return field.astype(jnp.float32).reshape(channels, height // 2, 2, width_cells // 2, 2)


def pooled(field):
    return jnp.mean(block_view(field), axis=(2, 4)).astype(jnp.bfloat16)


def block_sum(field):
    return jnp.sum(block_view(field), axis=(2, 4)).astype(jnp.bfloat16)


def upsampled(field):
    return jnp.repeat(jnp.repeat(field, 2, axis=1), 2, axis=2)


def gelu_back(preact, upstream):
    return jax.vjp(jax.nn.gelu, preact)[1](upstream)[0]


def fine_pad(field):
    return with_halo(field, (("rows", 1), ("cols", 2)), 1)


def coarse_pad(field):
    return with_halo(field, (("rows", 1), ("cols", 2)), 1)


def body(level_input, kernel_a, kernel_b, kernel_c, kernel_d, cotangent):
    padded_in = with_halo(level_input, (("rows", 1), ("cols", 2)), 1)
    padded_cot = None
    pre_a = conv_valid(padded_in, kernel_a)
    hidden = jax.nn.gelu(pre_a).astype(jnp.bfloat16)
    coarse = pooled(hidden)
    padded_coarse = coarse_pad(coarse)
    pre_b = conv_valid(padded_coarse, kernel_b)
    middle = jax.nn.gelu(pre_b).astype(jnp.bfloat16)
    padded_middle = coarse_pad(middle)
    coarse_out = conv_valid(padded_middle, kernel_c).astype(jnp.bfloat16)
    joined = (hidden.astype(jnp.float32) + upsampled(coarse_out).astype(jnp.float32)).astype(
        jnp.bfloat16
    )
    padded_joined = fine_pad(joined)
    result_field = conv_valid(padded_joined, kernel_d).astype(jnp.bfloat16)
    padded_cot = with_halo(cotangent, (("rows", 1), ("cols", 2)), 1)
    grad_joined = conv_valid(padded_cot, flipped(kernel_d)).astype(jnp.bfloat16)
    sum_d = kernel_grad(padded_joined, cotangent)
    grad_coarse = block_sum(grad_joined)
    sum_c = kernel_grad(padded_middle, grad_coarse)
    grad_pre_b = gelu_back(pre_b, conv_valid(coarse_pad(grad_coarse), flipped(kernel_c))).astype(
        jnp.bfloat16
    )
    sum_b = kernel_grad(padded_coarse, grad_pre_b)
    grad_pooled = conv_valid(coarse_pad(grad_pre_b), flipped(kernel_b)).astype(jnp.bfloat16)
    grad_hidden = grad_joined.astype(jnp.float32) + 0.25 * upsampled(grad_pooled).astype(
        jnp.float32
    )
    grad_pre_a = gelu_back(pre_a, grad_hidden).astype(jnp.bfloat16)
    input_grad = conv_valid(fine_pad(grad_pre_a), flipped(kernel_a)).astype(jnp.bfloat16)
    sum_a = kernel_grad(padded_in, grad_pre_a)
    sums = (sum_a, sum_b, sum_c, sum_d)
    flat = jnp.concatenate([s.reshape(-1, 128) for s in sums] + [jnp.zeros((320, 128), jnp.float32)])
    flat = reduce_all(flat.reshape(128, 16, 128)).reshape(2048, 128)
    start, totals = 0, []
    for s in sums:
        totals.append(flat[start : start + s.size // 128].reshape(s.shape))
        start += s.size // 128
    sum_a, sum_b, sum_c, sum_d = totals
    total_cells = (
        level_input.shape[1] * level_input.shape[2] * lax.axis_size("rows") * lax.axis_size("cols")
    )
    fine_scale = 1.0 / math.sqrt(total_cells)
    coarse_scale = 1.0 / math.sqrt(total_cells // 4)
    return (
        result_field,
        input_grad,
        sum_a * fine_scale,
        sum_b * coarse_scale,
        sum_c * coarse_scale,
        sum_d * fine_scale,
    )


def solution(mesh):
    placed = (P(None, "rows", "cols"), P(), P(), P(), P(), P(None, "rows", "cols"))
    return jax.shard_map(
        body,
        mesh=mesh,
        in_specs=placed,
        out_specs=(P(None, "rows", "cols"), P(None, "rows", "cols"), P(), P(), P(), P()),
        check_vma=False,
    )
```

```python
import math

import jax
import jax.numpy as jnp
from jax import lax
from jax.experimental import pallas as pl
from jax.experimental.pallas import tpu as pltpu
from jax.sharding import PartitionSpec as P

MESH = pl.DeviceIdType.MESH
BF, F32 = jnp.bfloat16, jnp.float32
VMEM = pl.BlockSpec(memory_space=pltpu.VMEM)
GELU_SCALE = 0.7978845608028654
GELU_CUBE = 0.044715
REACH = 7


def _pack_kernel(x_ref, cot_ref, rows_ref, left_ref, right_ref, flat):
    lane = lax.broadcasted_iota(jnp.int32, (64, 128), 1) // 8
    for field, ref in ((0, x_ref), (1, cot_ref)):
        flat[...] = ref[...].astype(F32).reshape(1024, 128)
        at = pl.ds(field * 64, 64)
        left = jnp.zeros((64, 128), F32)
        right = jnp.zeros((64, 128), F32)
        for h in range(16):
            row = flat[pl.ds(h, 64, stride=16), :]
            rows_ref[h, at, :] = row.astype(BF)
            left = jnp.where(lane == h, row if h == 0 else pltpu.roll(row, 8 * h, axis=1), left)
            right = jnp.where(lane == h, row if h == 15 else pltpu.roll(row, 8 * h + 8, axis=1), right)
        left_ref[at, :] = left.astype(BF)
        right_ref[at, :] = right.astype(BF)


def pack(level_input, cotangent):
    return pl.pallas_call(
        _pack_kernel,
        out_shape=(
            jax.ShapeDtypeStruct((16, 128, 128), BF),
            jax.ShapeDtypeStruct((128, 128), BF),
            jax.ShapeDtypeStruct((128, 128), BF),
        ),
        in_specs=[VMEM] * 2,
        out_specs=(VMEM,) * 3,
        scratch_shapes=[pltpu.VMEM((1024, 128), F32)],
        compiler_params=pltpu.CompilerParams(vmem_limit_bytes=16 * 1024 * 1024),
        cost_estimate=pl.CostEstimate(flops=1000000, bytes_accessed=1500000, transcendentals=0),
    )(level_input, cotangent)


def _rim_kernel(rows_ref, left_ref, right_ref, above_ref, below_ref, from_left_ref, from_right_ref,
                send_sem, recv_sem):
    row, col = lax.axis_index("rows"), lax.axis_index("cols")
    height, width = lax.axis_size("rows"), lax.axis_size("cols")

    def peer(dr, dc):
        return ((row + dr + height) % height, (col + dc + width) % width)

    around = [(dr, dc) for dr in (-1, 0, 1) for dc in (-1, 0, 1) if (dr, dc) != (0, 0)]
    barrier = pltpu.get_barrier_semaphore()
    for dr, dc in around:
        pl.semaphore_signal(barrier, inc=1, device_id=peer(dr, dc), device_id_type=MESH)
    pl.semaphore_wait(barrier, len(around))
    plan = [
        (rows_ref.at[pl.ds(0, REACH)], below_ref, (-1, 0)),
        (rows_ref.at[pl.ds(16 - REACH, REACH)], above_ref, (1, 0)),
    ]
    for dr in (0, -1, 1):
        plan.append((left_ref, from_right_ref.at[1 - dr], (dr, -1)))
        plan.append((right_ref, from_left_ref.at[1 - dr], (dr, 1)))
    copies = []
    for k, (src, dst, offset) in enumerate(plan):
        copies.append(pltpu.make_async_remote_copy(
            src_ref=src, dst_ref=dst, send_sem=send_sem.at[k], recv_sem=recv_sem.at[k],
            device_id=peer(*offset), device_id_type=MESH))
        copies[-1].start()
    for copy in copies:
        copy.wait()


def exchange(rows, left, right):
    shape = lambda n: jax.ShapeDtypeStruct((n, 128, 128), BF)
    return pl.pallas_call(
        _rim_kernel,
        out_shape=(shape(REACH), shape(REACH), shape(3), shape(3)),
        in_specs=[VMEM] * 3,
        out_specs=(VMEM,) * 4,
        scratch_shapes=[pltpu.SemaphoreType.DMA((8,)), pltpu.SemaphoreType.DMA((8,))],
        compiler_params=pltpu.CompilerParams(
            collective_id=0, has_side_effects=True, vmem_limit_bytes=16 * 1024 * 1024),
        cost_estimate=pl.CostEstimate(flops=1000, bytes_accessed=2000000, transcendentals=0),
    )(rows, left, right)


def _gelu_parts(x):
    square = x * x
    bend = jnp.tanh(GELU_SCALE * (x + GELU_CUBE * (x * square)))
    half = 0.5 + 0.5 * bend
    slope = half + (0.5 * GELU_SCALE) * x * (1.0 - bend * bend) * (1.0 + (3.0 * GELU_CUBE) * square)
    return x * half, slope


def _taps(x):
    lanes = x.shape[1]
    return jnp.concatenate(
        [pltpu.roll(x, 1, axis=1).astype(BF), x.astype(BF), pltpu.roll(x, lanes - 1, axis=1).astype(BF)],
        axis=0)


def _dot(a, b):
    return jnp.dot(a, b, preferred_element_type=F32)


def _dot_t(a, b):
    return lax.dot_general(a, b, (((1,), (1,)), ((), ())), preferred_element_type=F32)


def _loop(first, last, step, unroll=1):
    def body(i, carry):
        step(i)
        return carry
    lax.fori_loop(first, last, body, 0, unroll=unroll)


def _levels_kernel(edge_ref, rows_ref, above_ref, below_ref, from_left_ref, from_right_ref,
                   ka_ref, kb_ref, kc_ref, kd_ref, result_ref, input_grad_ref, sums_ref,
                   wa, wat, wb, wbt, wc, wct, wd, wdt, pool, spread,
                   x3, cot3, parts, cparts, hidden, slope_a, slope_b, coarse3, middle3, coarse_out,
                   joined3, grad_joined, grad_coarse3, grad_b3, grad_pool, up, grad_a3,
                   pad_a, pad_b, pad_c, pad_d, flat, acc):
    top, bottom = edge_ref[0], edge_ref[1]
    low, high = edge_ref[2], edge_ref[3]
    f_lane = lax.broadcasted_iota(jnp.int32, (1, 256), 1)
    c_lane = lax.broadcasted_iota(jnp.int32, (1, 128), 1)
    f_mask = ((f_lane < 136 - 8 * high) | (f_lane >= 248 + 8 * low)).astype(F32)
    c_mask = ((c_lane < 68 - 4 * high) | (c_lane >= 124 + 4 * low)).astype(F32)
    own_c = (c_lane < 64).astype(F32)

    for a in range(3):
        for b in range(3):
            tap, flip = 3 * a + b, 8 - (3 * a + b)
            at64, at128 = pl.ds(64 * a, 64), pl.ds(128 * a, 128)
            col64, col128 = slice(64 * b, 64 * b + 64), slice(128 * b, 128 * b + 128)
            wa[at64, col64] = ka_ref[tap]
            wd[at64, col64] = kd_ref[tap]
            wc[at64, col128] = kc_ref[tap]
            wbt[at64, col128] = kb_ref[flip]
            wat[at64, col64] = ka_ref[flip].astype(F32).T.astype(BF)
            wdt[at64, col64] = kd_ref[flip].astype(F32).T.astype(BF)
            wb[at128, col64] = kb_ref[tap].astype(F32).T.astype(BF)
            wct[at128, col64] = kc_ref[flip].astype(F32).T.astype(BF)
    cell = lax.broadcasted_iota(jnp.int32, (512, 128), 0)
    block = lax.broadcasted_iota(jnp.int32, (512, 128), 1)
    pool[...] = ((cell % 256) // 2 == block).astype(F32).astype(BF)
    cell = lax.broadcasted_iota(jnp.int32, (128, 256), 1)
    block = lax.broadcasted_iota(jnp.int32, (128, 256), 0)
    spread[...] = (cell // 2 == block).astype(F32).astype(BF)

    side_lane = lax.broadcasted_iota(jnp.int32, (128, 128), 1)
    for i in range(30):
        h = i - REACH
        if h < 0:
            center, j, p = above_ref[h + REACH], 0, h + 16
        elif h < 16:
            center, j, p = rows_ref[h], 1, h
        else:
            center, j, p = below_ref[h - 16], 2, h - 16
        right = from_right_ref[j].astype(F32)
        left = from_left_ref[j].astype(F32)
        right = right if p == 0 else pltpu.roll(right, 128 - 8 * p, axis=1)
        left = left if p == 15 else pltpu.roll(left, 120 - 8 * p, axis=1)
        side = jnp.where(side_lane < 8, right, left)
        wide = jnp.concatenate([center.astype(F32), side], axis=1) * f_mask
        x3[i] = _taps(wide[:64])
        cot3[i] = _taps(wide[64:])

    def clear(ref, top_rows, total):
        @pl.when(top == 1)
        def _():
            ref[pl.ds(0, top_rows)] = jnp.zeros((top_rows,) + ref.shape[1:], ref.dtype)

        @pl.when(bottom == 1)
        def _():
            ref[pl.ds(total - top_rows, top_rows)] = jnp.zeros((top_rows,) + ref.shape[1:], ref.dtype)

    clear(x3, 7, 30)
    clear(cot3, 7, 30)

    def conv(weights, source, into, rows, unroll):
        def step(i):
            into[i] = _dot(weights[...], source[i])
        _loop(0, rows, step, unroll)

    def gathered(from_, i, outs):
        return from_[i - 1, 0:outs] + from_[i, outs:2 * outs] + from_[i + 1, 2 * outs:3 * outs]

    conv(wa, x3, parts, 30, 5)

    def first(with_slope):
        def step(k):
            for s in range(2):
                pre = gathered(parts, 2 * k + 1 + s, 64)
                value, slope = _gelu_parts(pre)
                hidden[k, :, 256 * s:256 * s + 256] = (value * f_mask).astype(BF)
                if with_slope:
                    slope_a[k - 2, :, 256 * s:256 * s + 256] = slope
        return step
    _loop(0, 2, first(False))
    _loop(2, 12, first(True))
    _loop(12, 14, first(False))
    clear(hidden, 3, 14)

    def pool_step(k):
        coarse3[k] = _taps((_dot(hidden[k], pool[...]) * 0.25).astype(BF).astype(F32))
    _loop(0, 14, pool_step, 7)

    conv(wb, coarse3, cparts, 14, 7)

    def second(k):
        value, slope = _gelu_parts(gathered(cparts, k + 1, 128))
        middle3[k] = _taps(value * c_mask)
        slope_b[k] = slope
    _loop(0, 12, second, 2)
    clear(middle3, 2, 12)

    def third(k):
        cparts[k, 0:192] = _dot(wc[...], middle3[k])
    _loop(0, 12, third, 6)

    def third_sum(k):
        coarse_out[k] = (gathered(cparts, k + 1, 64) * c_mask).astype(BF)
    _loop(0, 10, third_sum, 5)
    clear(coarse_out, 1, 10)

    def spread_step(source):
        def step(k):
            up[k] = _dot(source[k], spread[...])
        return step
    _loop(0, 10, spread_step(coarse_out), 5)

    def join(k, s):
        both = hidden[k + 2, :, 256 * s:256 * s + 256].astype(F32) + up[k]
        joined3[2 * k - 1 + s] = _taps(both)[:, 0:128]
    join(0, 1)

    def join_step(k):
        join(k, 0)
        join(k, 1)
    _loop(1, 9, join_step, 2)
    join(9, 0)

    def out_rows(weights, source, ref):
        def step(i):
            parts[i, :, 0:128] = _dot(weights[...], source[i])
        _loop(0, 18, step, 6)
        for h in range(16):
            flat[pl.ds(h, 64, stride=16), :] = gathered(
                parts.at[:, :, pl.ds(0, 128)], h + 1, 64)
        ref[...] = flat[...].reshape(64, 16, 128).astype(BF)

    out_rows(wd, joined3, result_ref)

    conv(wdt, cot3, parts, 30, 5)

    def back_first(k):
        for s in range(2):
            grad = gathered(parts, 2 * k + 1 + s, 64) * f_mask
            grad_joined[k, :, 256 * s:256 * s + 256] = grad.astype(BF)
    _loop(0, 14, back_first, 2)
    clear(grad_joined, 3, 14)

    def back_pool(k):
        grad_coarse3[k] = _taps(_dot(grad_joined[k], pool[...]).astype(BF).astype(F32))
    _loop(0, 14, back_pool, 7)
    conv(wct, grad_coarse3, cparts, 14, 7)

    def back_second(k):
        grad_b3[k] = _taps(slope_b[k] * gathered(cparts, k + 1, 128) * c_mask)
    _loop(0, 12, back_second, 2)
    clear(grad_b3, 2, 12)

    def back_third(k):
        cparts[k, 0:192] = _dot(wbt[...], grad_b3[k])
    _loop(0, 12, back_third, 6)

    def back_third_sum(k):
        grad_pool[k] = gathered(cparts, k + 1, 64).astype(BF)
    _loop(0, 10, back_third_sum, 5)
    _loop(0, 10, spread_step(grad_pool), 5)

    def back_join(k, s):
        at = slice(256 * s, 256 * s + 256)
        grad = grad_joined[k + 2, :, at].astype(F32) + 0.25 * up[k]
        grad_a3[2 * k - 1 + s] = _taps(slope_a[k, :, at] * grad * f_mask)[:, 0:128]
    back_join(0, 1)

    def back_join_step(k):
        back_join(k, 0)
        back_join(k, 1)
    _loop(1, 9, back_join_step, 2)
    back_join(9, 0)
    clear(grad_a3, 1, 18)
    out_rows(wat, grad_a3, input_grad_ref)

    for pad, before in ((pad_a, 2), (pad_d, 2), (pad_c, 2)):
        pad[pl.ds(0, before)] = jnp.zeros((before,) + pad.shape[1:], BF)
        size = pad.shape[0]
        pad[pl.ds(size - before, before)] = jnp.zeros((before,) + pad.shape[1:], BF)
    _loop(0, 16, lambda h: pad_a.__setitem__(h + 2, grad_a3[h + 1, 64:128, :]), 4)
    _loop(0, 16, lambda h: pad_d.__setitem__(h + 2, cot3[h + 7, 64:128, 0:128]), 4)
    _loop(0, 8, lambda k: pad_b.__setitem__(
        k, (grad_b3[k + 2, 128:256, :].astype(F32) * own_c).astype(BF)), 4)
    _loop(0, 8, lambda k: pad_c.__setitem__(
        k + 2, (grad_coarse3[k + 3, 64:128, :].astype(F32) * own_c).astype(BF)), 4)

    def stacked(pad, j):
        return jnp.concatenate([pad[j + 2], pad[j + 1], pad[j]], axis=0)

    def pair(one, j):
        return jnp.concatenate([one(2 * j), one(2 * j + 1)], axis=1)

    def weight_grad(pad, window, pairs, into):
        def step(j):
            into[...] += _dot_t(pair(lambda i: stacked(pad, i), j), pair(window, j))
        into[...] = jnp.zeros(into.shape, F32)
        _loop(0, pairs, step, pairs)

    sums_ref[pl.ds(1728, 320), :] = jnp.zeros((320, 128), F32)
    acc_a, acc_d = acc.at[0:192, 0:192], acc.at[0:192, 256:448]
    acc_a = acc.at[pl.ds(0, 192), pl.ds(0, 256)]
    acc_d = acc.at[pl.ds(0, 192), pl.ds(256, 256)]
    for pad, window, at in ((pad_a, lambda i: x3[i + 6, :, 0:128], 0),
                            (pad_d, lambda i: joined3[i], 256)):
        def step(j, pad=pad, window=window, at=at):
            acc[0:192, at:at + 192] += _dot_t(pair(lambda i: stacked(pad, i), j), pair(window, j))
        acc[0:192, at:at + 192] = jnp.zeros((192, 192), F32)
        _loop(0, 9, step, 3)
    for a in range(3):
        for b in range(3):
            rows = slice(64 * a, 64 * a + 64)
            sums_ref[pl.ds(64 * (3 * a + b), 64), :] = jnp.concatenate(
                [acc[rows, 64 * b:64 * b + 64], acc[rows, 256 + 64 * b:320 + 64 * b]], axis=1)

    sums_ref[pl.ds(576, 576), :] = jnp.zeros((576, 128), F32)

    def b_step(j):
        def window(k):
            return jnp.concatenate([coarse3[k + 2], coarse3[k + 3], coarse3[k + 4]], axis=0)
        sums_ref[pl.ds(576, 576), :] += _dot_t(pair(window, j), pair(lambda k: pad_b[k], j))
    _loop(0, 4, b_step, 2)

    acc[0:192, 0:384] = jnp.zeros((192, 384), F32)

    def c_step(j):
        acc[0:192, 0:384] += _dot_t(
            pair(lambda i: stacked(pad_c, i), j), pair(lambda i: middle3[i + 1], j))
    _loop(0, 5, c_step, 1)
    for a in range(3):
        for b in range(3):
            sums_ref[pl.ds(1152 + 64 * (3 * a + b), 64), :] = acc[64 * a:64 * a + 64, 128 * b:128 * b + 128]


def levels(edges, rows, above, below, from_left, from_right, ka, kb, kc, kd):
    scratch = [
        ((192, 192), BF), ((192, 192), BF), ((384, 192), BF), ((192, 384), BF),
        ((192, 384), BF), ((384, 192), BF), ((192, 192), BF), ((192, 192), BF),
        ((512, 128), BF), ((128, 256), BF),
        ((30, 192, 256), BF), ((30, 192, 256), BF), ((30, 192, 256), F32), ((14, 384, 128), F32),
        ((14, 64, 512), BF), ((10, 64, 512), F32), ((12, 128, 128), F32),
        ((14, 192, 128), BF), ((12, 384, 128), BF), ((10, 64, 128), BF),
        ((18, 192, 128), BF), ((14, 64, 512), BF), ((14, 192, 128), BF), ((12, 384, 128), BF),
        ((10, 64, 128), BF), ((10, 64, 256), F32), ((18, 192, 128), BF),
        ((20, 64, 128), BF), ((8, 128, 128), BF), ((12, 64, 128), BF), ((20, 64, 128), BF),
        ((1024, 128), F32), ((192, 512), F32),
    ]
    return pl.pallas_call(
        _levels_kernel,
        out_shape=(
            jax.ShapeDtypeStruct((64, 16, 128), BF),
            jax.ShapeDtypeStruct((64, 16, 128), BF),
            jax.ShapeDtypeStruct((2048, 128), F32),
        ),
        in_specs=[pl.BlockSpec(memory_space=pltpu.SMEM)] + [VMEM] * 9,
        out_specs=(VMEM,) * 3,
        scratch_shapes=[pltpu.VMEM(shape, dtype) for shape, dtype in scratch],
        compiler_params=pltpu.CompilerParams(vmem_limit_bytes=48 * 1024 * 1024),
        cost_estimate=pl.CostEstimate(flops=2000000000, bytes_accessed=8000000, transcendentals=1000000),
    )(edges, rows, above, below, from_left, from_right, ka, kb, kc, kd)


def _reduce_kernel(x_ref, out_ref, pair_out, pair_in, plane_out, plane_in, own, near_in, far, whole,
                   pair_s, pair_r, plane_s, plane_r, near_s, near_r, far_s, far_r,
                   gnear_s, gnear_r, gplane_s, gplane_r, gpair_s, gpair_r):
    rows, cols = lax.axis_index("rows"), lax.axis_index("cols")
    y, near, core = rows // 8, (rows // 2) % 4, rows % 2
    far_at, x = cols // 4, cols % 4

    def place(y_at, near_at, core_at, z_at, x_at):
        return (y_at * 8 + near_at * 2 + core_at, z_at * 4 + x_at)

    partner = place(y, near, 1 - core, far_at, x)

    def plane_peer(dy, dx):
        return place((y + dy) % 4, near, core, far_at, (x + dx) % 4)

    def near_peer(dz):
        return place(y, (near + dz) % 4, core, far_at, x)

    def far_peer(dz):
        return place(y, near, core, (far_at + dz) % 4, x)

    plane_steps = [(dy, dx) for dy in (2, 1, 3, 0) for dx in (2, 1, 3, 0)]
    barrier = pltpu.get_barrier_semaphore()
    greeted = [partner]
    greeted += [plane_peer(dy, dx) for dy, dx in plane_steps if (dy, dx) != (0, 0)]
    greeted += [near_peer(dz) for dz in (1, 2, 3)] + [far_peer(dz) for dz in (1, 2, 3)]
    for peer in greeted:
        pl.semaphore_signal(barrier, inc=1, device_id=peer, device_id_type=MESH)

    def send(src, dst, send_sem, recv_sem, peer):
        copy = pltpu.make_async_remote_copy(
            src_ref=src, dst_ref=dst, send_sem=send_sem, recv_sem=recv_sem,
            device_id=peer, device_id_type=MESH)
        copy.start()
        return copy

    theirs, mine = (1 - core) * 64, core * 64
    started = []
    for dy in (2, 1, 3, 0):
        first = ((y + dy) % 4) * 16
        pair_out[pl.ds(first, 16)] = x_ref[pl.ds(theirs + first, 16)].astype(jnp.bfloat16)
    pl.semaphore_wait(barrier, len(greeted))
    pair = {}
    for dy in (2, 1, 3, 0):
        piece = pl.ds(((y + dy) % 4) * 16, 16)
        pair[dy] = send(pair_out.at[piece], pair_in.at[piece], pair_s.at[dy], pair_r.at[dy], partner)
    plane = {}
    for dy, dx in plane_steps:
        if dx == 2:
            pair[dy].wait_recv()
        first = ((y + dy) % 4) * 16 + ((x + dx) % 4) * 4
        chunk = pl.ds(first, 4)
        both = x_ref[pl.ds(mine + first, 4)] + pair_in[chunk].astype(jnp.float32)
        if (dy, dx) == (0, 0):
            own[...] = both
        else:
            k = dy * 4 + dx
            plane_out[chunk] = both.astype(jnp.bfloat16)
            plane[k] = send(plane_out.at[chunk], plane_in.at[k], plane_s.at[k], plane_r.at[k],
                            plane_peer(dy, dx))
    total = own[...]
    for k in (4, 12, 1, 3, 8, 2, 5, 7, 13, 15, 6, 14, 9, 11, 10):
        plane[k].wait_recv()
        total = total + plane_in[k].astype(jnp.float32)
    own[...] = total
    near_copies = {}
    for dz in (2, 1, 3):
        near_copies[dz] = send(own.at[(near + dz) % 4], near_in.at[dz], near_s.at[dz],
                               near_r.at[dz], near_peer(dz))
    tile = own[near]
    for dz in (1, 3, 2):
        near_copies[dz].wait_recv()
        tile = tile + near_in[dz]
    far[far_at] = tile
    far_copies = {}
    for dz in (2, 1, 3):
        far_copies[dz] = send(far.at[far_at], far.at[far_at], far_s.at[dz], far_r.at[dz], far_peer(dz))
    for dz in (1, 3, 2):
        far_copies[dz].wait_recv()
    tile = ((far[0] + far[1]) + far[2]) + far[3]
    base = mine + y * 16 + x * 4
    whole[base + near] = tile.astype(jnp.bfloat16)
    gather = []
    for dz in (2, 1, 3):
        at = whole.at[base + near]
        gather.append(send(at, at, gnear_s.at[dz], gnear_r.at[dz], near_peer(dz)))
    for copy in gather:
        copy.wait_recv()
    gplane = {}
    for dy, dx in plane_steps:
        if (dy, dx) != (0, 0):
            k = dy * 4 + dx
            at = whole.at[pl.ds(base, 4)]
            gplane[k] = send(at, at, gplane_s.at[k], gplane_r.at[k], plane_peer(dy, dx))
    gpair = []
    for dy in (0, 1, 3, 2):
        for dx in (0, 1, 3, 2):
            if (dy, dx) != (0, 0):
                gplane[dy * 4 + dx].wait_recv()
        at = whole.at[pl.ds(mine + ((y - dy + 4) % 4) * 16, 16)]
        gpair.append(send(at, at, gpair_s.at[dy], gpair_r.at[dy], partner))
    for copy in gpair:
        copy.wait_recv()
    out_ref[...] = whole[...].astype(jnp.float32)
    for copies in (pair.values(), plane.values(), near_copies.values(), far_copies.values(), gather,
                   gplane.values(), gpair):
        for copy in copies:
            copy.wait_send()


def reduce_all(tiles):
    dma = pltpu.SemaphoreType.DMA
    return pl.pallas_call(
        _reduce_kernel,
        out_shape=jax.ShapeDtypeStruct((128, 16, 128), jnp.float32),
        in_specs=[pl.BlockSpec(memory_space=pltpu.VMEM)],
        out_specs=pl.BlockSpec(memory_space=pltpu.VMEM),
        scratch_shapes=[
            pltpu.VMEM((64, 16, 128), jnp.bfloat16),
            pltpu.VMEM((64, 16, 128), jnp.bfloat16),
            pltpu.VMEM((64, 16, 128), jnp.bfloat16),
            pltpu.VMEM((16, 4, 16, 128), jnp.bfloat16),
            pltpu.VMEM((4, 16, 128), jnp.float32),
            pltpu.VMEM((4, 16, 128), jnp.float32),
            pltpu.VMEM((4, 16, 128), jnp.float32),
            pltpu.VMEM((128, 16, 128), jnp.bfloat16),
            dma((4,)), dma((4,)), dma((16,)), dma((16,)), dma((4,)), dma((4,)), dma((4,)), dma((4,)),
            dma((4,)), dma((4,)), dma((16,)), dma((16,)), dma((4,)), dma((4,)),
        ],
        compiler_params=pltpu.CompilerParams(
            collective_id=1, has_side_effects=True, vmem_limit_bytes=32 * 1024 * 1024),
        cost_estimate=pl.CostEstimate(flops=1000000, bytes_accessed=4000000, transcendentals=0),
    )(tiles)


def tap_major(kernel, order):
    taps = jnp.transpose(kernel, (2, 3) + order)
    return taps.reshape((9,) + taps.shape[2:])


def body(level_input, kernel_a, kernel_b, kernel_c, kernel_d, cotangent):
    row, col = lax.axis_index("rows"), lax.axis_index("cols")
    last_row, last_col = lax.axis_size("rows") - 1, lax.axis_size("cols") - 1
    edges = jnp.stack([row == 0, row == last_row, col == 0, col == last_col]).astype(jnp.int32)
    rows, left, right = pack(level_input, cotangent)
    above, below, from_left, from_right = exchange(rows, left, right)
    result_field, input_grad, sums = levels(
        edges, rows, above, below, from_left, from_right,
        tap_major(kernel_a, (0, 1)), tap_major(kernel_b, (1, 0)),
        tap_major(kernel_c, (0, 1)), tap_major(kernel_d, (0, 1)))
    sums = reduce_all(sums.reshape(128, 16, 128)).reshape(2048, 128)
    both = sums[0:576].reshape(3, 3, 64, 128)
    grad_b = sums[576:1152].reshape(3, 3, 64, 128)
    grad_c = sums[1152:1728].reshape(3, 3, 64, 128)
    total_cells = (
        level_input.shape[1] * level_input.shape[2] * lax.axis_size("rows") * lax.axis_size("cols")
    )
    fine_scale = 1.0 / math.sqrt(total_cells)
    coarse_scale = 1.0 / math.sqrt(total_cells // 4)
    return (
        result_field,
        input_grad,
        jnp.transpose(both[..., :64] * fine_scale, (2, 3, 0, 1)),
        jnp.transpose(grad_b * coarse_scale, (3, 2, 0, 1)),
        jnp.transpose(grad_c * coarse_scale, (2, 3, 0, 1)),
        jnp.transpose(both[..., 64:] * fine_scale, (2, 3, 0, 1)),
    )


def solution(mesh):
    placed = (P(None, "rows", "cols"), P(), P(), P(), P(), P(None, "rows", "cols"))
    return jax.shard_map(
        body,
        mesh=mesh,
        in_specs=placed,
        out_specs=(P(None, "rows", "cols"), P(None, "rows", "cols"), P(), P(), P(), P()),
        check_vma=False,
    )
```

```python
import functools
import math

import jax
import jax.numpy as jnp
from jax import lax
from jax.experimental import pallas as pl
from jax.experimental.pallas import tpu as pltpu
from jax.sharding import PartitionSpec as P

MESH = pl.DeviceIdType.MESH
BF, F32 = jnp.bfloat16, jnp.float32
VMEM = pl.BlockSpec(memory_space=pltpu.VMEM)
GELU_SCALE = 0.7978845608028654
GELU_CUBE = 0.044715
REACH = 7


def _gelu_parts(x):
    square = x * x
    bend = jnp.tanh(GELU_SCALE * (x + GELU_CUBE * (x * square)))
    half = 0.5 + 0.5 * bend
    slope = half + (0.5 * GELU_SCALE) * x * (1.0 - bend * bend) * (1.0 + (3.0 * GELU_CUBE) * square)
    return x * half, slope


def _taps(x):
    lanes = x.shape[1]
    return jnp.concatenate(
        [pltpu.roll(x, 1, axis=1).astype(BF), x.astype(BF), pltpu.roll(x, lanes - 1, axis=1).astype(BF)],
        axis=0)


def _dot(a, b):
    return jnp.dot(a, b, preferred_element_type=F32)


def _dot_t(a, b):
    return lax.dot_general(a, b, (((1,), (1,)), ((), ())), preferred_element_type=F32)


def _loop(first, last, step, unroll=1):
    def body(i, carry):
        step(i)
        return carry
    lax.fori_loop(first, last, body, 0, unroll=unroll)


class _Sum:
    def __init__(self, whole, src, *rest):
        self.whole, self.src, self.sems = whole, src, rest[6:]
        (self.pair_out, self.pair_in, self.plane_out, self.plane_in, self.near_all, self.far_all) = rest[:6]
        self.half = src.shape[0] // 2
        self.piece, self.chunk = self.half // 4, self.half // 16
        rows, cols = lax.axis_index("rows"), lax.axis_index("cols")
        self.y, self.near, self.core = rows // 8, (rows // 2) % 4, rows % 2
        self.far_at, self.x = cols // 4, cols % 4
        self.partner = self.place(1 - self.core, 0, 0, 0, 0)
        self.steps = [(dy, dx) for dy in (2, 1, 3, 0) for dx in (2, 1, 3, 0)]
        self.base = self.core * self.half + self.y * self.piece + self.x * self.chunk
        self.started = []

    def place(self, core, dy, dx, dn, df):
        return (((self.y + dy) % 4) * 8 + ((self.near + dn) % 4) * 2 + core,
                ((self.far_at + df) % 4) * 4 + (self.x + dx) % 4)

    def peers(self):
        found = [self.partner]
        found += [self.place(self.core, dy, dx, 0, 0) for dy, dx in self.steps if (dy, dx) != (0, 0)]
        found += [self.place(self.core, 0, 0, d, 0) for d in (1, 2, 3)]
        found += [self.place(self.core, 0, 0, 0, d) for d in (1, 2, 3)]
        return found

    def send(self, src, dst, phase, k, peer):
        copy = pltpu.make_async_remote_copy(
            src_ref=src, dst_ref=dst, send_sem=self.sems[2 * phase].at[k],
            recv_sem=self.sems[2 * phase + 1].at[k], device_id=peer, device_id_type=MESH)
        copy.start()
        self.started.append(copy)
        return copy

    def pair(self):
        self.copies = {}
        theirs = (1 - self.core) * self.half
        for dy in (2, 1, 3, 0):
            first = ((self.y + dy) % 4) * self.piece
            piece = pl.ds(first, self.piece)
            self.pair_out[piece] = self.src[pl.ds(theirs + first, self.piece)].astype(BF)
            self.copies[dy] = self.send(
                self.pair_out.at[piece], self.pair_in.at[piece], 0, dy, self.partner)

    def plane(self):
        mine, pair, self.copies = self.core * self.half, self.copies, {}
        for dy, dx in self.steps:
            if dx == 2:
                pair[dy].wait_recv()
            first = ((self.y + dy) % 4) * self.piece + ((self.x + dx) % 4) * self.chunk
            chunk = pl.ds(first, self.chunk)
            both = self.src[pl.ds(mine + first, self.chunk)] + self.pair_in[chunk].astype(F32)
            if (dy, dx) == (0, 0):
                self.own = both
            else:
                k = dy * 4 + dx
                self.plane_out[chunk] = both.astype(BF)
                self.copies[k] = self.send(
                    self.plane_out.at[chunk], self.plane_in.at[k], 1, k,
                    self.place(self.core, dy, dx, 0, 0))

    def along_near(self):
        total = self.own
        for k in (4, 12, 1, 3, 8, 2, 5, 7, 13, 15, 6, 14, 9, 11, 10):
            self.copies[k].wait_recv()
            total = total + self.plane_in[k].astype(F32)
        self.near_all[self.near] = total
        at = self.near_all.at[self.near]
        self.copies = {}
        for d in (2, 1, 3):
            self.copies[d] = self.send(at, at, 2, d, self.place(self.core, 0, 0, d, 0))

    def along_far(self):
        for d in (1, 3, 2):
            self.copies[d].wait_recv()
        near = self.near_all
        self.far_all[self.far_at] = ((near[0] + near[1]) + near[2]) + near[3]
        at = self.far_all.at[self.far_at]
        self.copies = {}
        for d in (2, 1, 3):
            self.copies[d] = self.send(at, at, 3, d, self.place(self.core, 0, 0, 0, d))

    def back_plane(self):
        for d in (1, 3, 2):
            self.copies[d].wait_recv()
        far, chunk = self.far_all, pl.ds(self.base, self.chunk)
        self.whole[chunk] = (((far[0] + far[1]) + far[2]) + far[3]).astype(BF)
        at = self.whole.at[chunk]
        self.copies = {}
        for dy, dx in self.steps:
            if (dy, dx) != (0, 0):
                k = dy * 4 + dx
                self.copies[k] = self.send(at, at, 4, k, self.place(self.core, dy, dx, 0, 0))

    def back_pair(self):
        plane, self.copies = self.copies, {}
        for dy in (0, 1, 3, 2):
            for dx in (0, 1, 3, 2):
                if (dy, dx) != (0, 0):
                    plane[dy * 4 + dx].wait_recv()
            first = self.core * self.half + ((self.y - dy + 4) % 4) * self.piece
            at = self.whole.at[pl.ds(first, self.piece)]
            self.copies[dy] = self.send(at, at, 5, dy, self.partner)

    def finish(self):
        for dy in (0, 1, 3, 2):
            self.copies[dy].wait_recv()
        for copy in self.started:
            copy.wait_send()


def _levels_kernel(x_at, cot_at, ka_at, kb_at, kc_at, kd_at,
                   result_ref, input_grad_ref, early_out, late_out,
                   x_ref, cot_ref, ka_ref, kb_ref, kc_ref, kd_ref,
                   rows_ref, left_ref, right_ref, above_ref, below_ref, from_left_ref, from_right_ref,
                   up_corners, down_corners, above_corners, below_corners,
                   wa, wat, wb, wbt, wc, wct, wd, wdt, pool, spread,
                   x3, cot3, parts, cot_parts, cparts, hidden, slope_a, slope_b, coarse3, middle3,
                   coarse_out, joined3, grad_joined, grad_coarse3, grad_b3, grad_pool, up, grad_a3,
                   pad_a, pad_b, pad_c, pad_d, flat, acc, *rest):
    load_sem, rim_send, rim_recv = rest[:3]
    early_rest, late_rest = rest[3:23], rest[23:43]
    row, col = lax.axis_index("rows"), lax.axis_index("cols")
    height, width = lax.axis_size("rows"), lax.axis_size("cols")
    top = (row == 0).astype(jnp.int32)
    bottom = (row == height - 1).astype(jnp.int32)
    low = (col == 0).astype(jnp.int32)
    high = (col == width - 1).astype(jnp.int32)

    early, late = _Sum(*early_rest), _Sum(*late_rest)
    early_src, late_src = early.src, late.src

    def beside(dr, dc):
        return ((row + dr + height) % height, (col + dc + width) % width)

    around = [(0, -1), (0, 1), (-1, 0), (1, 0)]
    greeted = [beside(dr, dc) for dr, dc in around] + early.peers()
    barrier = pltpu.get_barrier_semaphore()
    for peer in greeted:
        pl.semaphore_signal(barrier, inc=1, device_id=peer, device_id_type=MESH)
    loads = [
        pltpu.make_async_copy(src, dst, load_sem.at[k]) for k, (src, dst) in enumerate((
            (x_at, x_ref), (cot_at, cot_ref), (ka_at, ka_ref), (kb_at, kb_ref), (kc_at, kc_ref), (kd_at, kd_ref)))]
    for load in loads:
        load.start()

    lane = lax.broadcasted_iota(jnp.int32, (64, 128), 1) // 8
    for field, ref in ((0, x_ref), (1, cot_ref)):
        loads[field].wait()
        flat[...] = ref[...].astype(F32).reshape(1024, 128)
        at = pl.ds(field * 64, 64)
        left = jnp.zeros((64, 128), F32)
        right = jnp.zeros((64, 128), F32)
        for h in range(16):
            line = flat[pl.ds(h, 64, stride=16), :]
            rows_ref[h, at, :] = line.astype(BF)
            left = jnp.where(lane == h, line if h == 0 else pltpu.roll(line, 8 * h, axis=1), left)
            right = jnp.where(lane == h, line if h == 15 else pltpu.roll(line, 8 * h + 8, axis=1), right)
        left_ref[at, :] = left.astype(BF)
        right_ref[at, :] = right.astype(BF)
    pl.semaphore_wait(barrier, len(greeted))
    rim = []

    def push(src, dst, offset):
        rim.append(pltpu.make_async_remote_copy(
            src_ref=src, dst_ref=dst, send_sem=rim_send.at[len(rim)], recv_sem=rim_recv.at[len(rim)],
            device_id=beside(*offset), device_id_type=MESH))
        rim[-1].start()

    push(left_ref, from_right_ref, (0, -1))
    push(right_ref, from_left_ref, (0, 1))
    push(rows_ref.at[pl.ds(0, REACH)], below_ref, (-1, 0))
    push(rows_ref.at[pl.ds(16 - REACH, REACH)], above_ref, (1, 0))
    f_lane = lax.broadcasted_iota(jnp.int32, (1, 256), 1)
    c_lane = lax.broadcasted_iota(jnp.int32, (1, 128), 1)
    f_mask = ((f_lane < 136 - 8 * high) | (f_lane >= 248 + 8 * low)).astype(F32)
    c_mask = ((c_lane < 68 - 4 * high) | (c_lane >= 124 + 4 * low)).astype(F32)
    own_c = (c_lane < 64).astype(F32)

    for load in loads[2:]:
        load.wait()
    for a in range(3):
        for b in range(3):
            tap, flip = 3 * a + b, 8 - (3 * a + b)
            at64, at128 = pl.ds(64 * a, 64), pl.ds(128 * a, 128)
            col64, col128 = slice(64 * b, 64 * b + 64), slice(128 * b, 128 * b + 128)
            wa[at64, col64] = ka_ref[tap]
            wd[at64, col64] = kd_ref[tap]
            wc[at64, col128] = kc_ref[tap]
            wbt[at64, col128] = kb_ref[flip]
            wat[at64, col64] = ka_ref[flip].astype(F32).T.astype(BF)
            wdt[at64, col64] = kd_ref[flip].astype(F32).T.astype(BF)
            wb[at128, col64] = kb_ref[tap].astype(F32).T.astype(BF)
            wct[at128, col64] = kc_ref[flip].astype(F32).T.astype(BF)
    cell = lax.broadcasted_iota(jnp.int32, (512, 128), 0)
    block = lax.broadcasted_iota(jnp.int32, (512, 128), 1)
    pool[...] = ((cell % 256) // 2 == block).astype(F32).astype(BF)
    cell = lax.broadcasted_iota(jnp.int32, (128, 256), 1)
    block = lax.broadcasted_iota(jnp.int32, (128, 256), 0)
    spread[...] = (cell // 2 == block).astype(F32).astype(BF)

    side_lane = lax.broadcasted_iota(jnp.int32, (128, 128), 1)

    def unpack(i):
        h = i - REACH
        if h < 0:
            center, left, right, p = above_ref[h + REACH], above_corners[...], above_corners[...], h + 16
            turn_left, turn_right = (184 - 8 * p) % 128, 128 - 8 * p
        elif h < 16:
            center, left, right, p = rows_ref[h], from_left_ref[...], from_right_ref[...], h
            turn_left, turn_right = 120 - 8 * p, (128 - 8 * p) % 128
        else:
            center, left, right, p = below_ref[h - 16], below_corners[...], below_corners[...], h - 16
            turn_left, turn_right = 120 - 8 * p, 64 - 8 * p
        left, right = left.astype(F32), right.astype(F32)
        right = pltpu.roll(right, turn_right, axis=1) if turn_right else right
        left = pltpu.roll(left, turn_left, axis=1) if turn_left else left
        side = jnp.where(side_lane < 8, right, left)
        wide = jnp.concatenate([center.astype(F32), side], axis=1) * f_mask
        x3[i] = _taps(wide[:64])
        cot3[i] = _taps(wide[64:])

    def conv(weights, source, into, first, last, unroll):
        def step(i):
            into[i] = _dot(weights[...], source[i])
        _loop(first, last, step, unroll)

    rim[0].wait_recv()
    rim[1].wait_recv()
    left, right = from_left_ref[...].astype(F32), from_right_ref[...].astype(F32)
    up_corners[...] = jnp.where(side_lane < 64, left, pltpu.roll(right, 64, axis=1)).astype(BF)
    down_corners[...] = jnp.where(side_lane < 64, pltpu.roll(left, 64, axis=1), right).astype(BF)
    push(up_corners, below_corners, (-1, 0))
    push(down_corners, above_corners, (1, 0))
    for i in range(REACH, REACH + 16):
        unpack(i)
    conv(wa, x3, parts, 7, 23, 4)
    conv(wdt, cot3, cot_parts, 7, 23, 4)
    for copy in rim[2:]:
        copy.wait_recv()
    for i in list(range(REACH)) + list(range(REACH + 16, 30)):
        unpack(i)

    def clear(ref, top_rows, total):
        @pl.when(top == 1)
        def _():
            ref[pl.ds(0, top_rows)] = jnp.zeros((top_rows,) + ref.shape[1:], ref.dtype)

        @pl.when(bottom == 1)
        def _():
            ref[pl.ds(total - top_rows, top_rows)] = jnp.zeros((top_rows,) + ref.shape[1:], ref.dtype)

    clear(x3, 7, 30)
    clear(cot3, 7, 30)

    def gathered(from_, i, outs):
        return from_[i - 1, 0:outs] + from_[i, outs:2 * outs] + from_[i + 1, 2 * outs:3 * outs]

    for first_row in (0, 23):
        conv(wa, x3, parts, first_row, first_row + 7, 7)
        conv(wdt, cot3, cot_parts, first_row, first_row + 7, 7)

    def first(with_slope):
        def step(k):
            for s in range(2):
                pre = gathered(parts, 2 * k + 1 + s, 64)
                value, slope = _gelu_parts(pre)
                hidden[k, :, 256 * s:256 * s + 256] = (value * f_mask).astype(BF)
                if with_slope:
                    slope_a[k - 2, :, 256 * s:256 * s + 256] = slope
        return step
    _loop(0, 2, first(False))
    _loop(2, 12, first(True))
    _loop(12, 14, first(False))
    clear(hidden, 3, 14)

    def pool_step(k):
        coarse3[k] = _taps((_dot(hidden[k], pool[...]) * 0.25).astype(BF).astype(F32))
    _loop(0, 14, pool_step, 7)

    conv(wb, coarse3, cparts, 0, 14, 7)

    def second(k):
        value, slope = _gelu_parts(gathered(cparts, k + 1, 128))
        middle3[k] = _taps(value * c_mask)
        slope_b[k] = slope
    _loop(0, 12, second, 2)
    clear(middle3, 2, 12)

    def third(k):
        cparts[k, 0:192] = _dot(wc[...], middle3[k])
    _loop(0, 12, third, 6)

    def third_sum(k):
        coarse_out[k] = (gathered(cparts, k + 1, 64) * c_mask).astype(BF)
    _loop(0, 10, third_sum, 5)
    clear(coarse_out, 1, 10)

    def spread_step(source):
        def step(k):
            up[k] = _dot(source[k], spread[...])
        return step
    _loop(0, 10, spread_step(coarse_out), 5)

    def join(k, s):
        both = hidden[k + 2, :, 256 * s:256 * s + 256].astype(F32) + up[k]
        joined3[2 * k - 1 + s] = _taps(both)[:, 0:128]
    join(0, 1)

    def join_step(k):
        join(k, 0)
        join(k, 1)
    _loop(1, 9, join_step, 2)
    join(9, 0)

    def out_parts(weights, source):
        def step(i):
            parts[i, :, 0:128] = _dot(weights[...], source[i])
        _loop(0, 18, step, 6)

    def out_rows(ref):
        for h in range(16):
            flat[pl.ds(h, 64, stride=16), :] = gathered(
                parts.at[:, :, pl.ds(0, 128)], h + 1, 64)
        ref[...] = flat[...].reshape(64, 16, 128).astype(BF)

    out_parts(wd, joined3)
    out_rows(result_ref)

    def stacked(pad, j):
        return jnp.concatenate([pad[j + 2], pad[j + 1], pad[j]], axis=0)

    def pair(one, j):
        return jnp.concatenate([one(2 * j), one(2 * j + 1)], axis=1)

    def framed(pad, first, count, own):
        pad[pl.ds(0, 2)] = jnp.zeros((2,) + pad.shape[1:], BF)
        pad[pl.ds(count + 2, 2)] = jnp.zeros((2,) + pad.shape[1:], BF)

        def step(h):
            pad[h + 2] = own(h + first)
        _loop(0, count, step, 4)

    def fine_weight_grad(pad, window, src, first):
        acc[0:192, 0:192] = jnp.zeros((192, 192), F32)

        def step(j):
            acc[0:192, 0:192] += _dot_t(pair(lambda i: stacked(pad, i), j), pair(window, j))
        _loop(0, 9, step, 3)

        def tap(t):
            if t > 8:
                return jnp.zeros((64, 64), F32)
            a, b = t // 3, t % 3
            return acc[64 * a:64 * a + 64, 64 * b:64 * b + 64]
        for t in range(5):
            both = jnp.concatenate([tap(t), tap(t + 5)], axis=1)
            src[pl.ds(first + 4 * t, 4)] = both.reshape(4, 16, 128)

    framed(pad_d, 7, 16, lambda h: cot3[h, 64:128, 0:128])
    fine_weight_grad(pad_d, lambda i: joined3[i], early_src, 36)


    def back_first(k):
        for s in range(2):
            grad = gathered(cot_parts, 2 * k + 1 + s, 64) * f_mask
            grad_joined[k, :, 256 * s:256 * s + 256] = grad.astype(BF)
    _loop(0, 14, back_first, 2)
    clear(grad_joined, 3, 14)

    def back_pool(k):
        grad_coarse3[k] = _taps(_dot(grad_joined[k], pool[...]).astype(BF).astype(F32))
    _loop(0, 14, back_pool, 7)

    framed(pad_c, 3, 8, lambda k: (grad_coarse3[k, 64:128, :].astype(F32) * own_c).astype(BF))
    acc[0:192, 0:384] = jnp.zeros((192, 384), F32)

    def c_step(j):
        acc[0:192, 0:384] += _dot_t(
            pair(lambda i: stacked(pad_c, i), j), pair(lambda i: middle3[i + 1], j))
    _loop(0, 5, c_step, 1)
    for a in range(3):
        for b in range(3):
            early_src[pl.ds(4 * (3 * a + b), 4)] = acc[
                64 * a:64 * a + 64, 128 * b:128 * b + 128].reshape(4, 16, 128)
    conv(wct, grad_coarse3, cparts, 0, 14, 7)

    def back_second(k):
        grad_b3[k] = _taps(slope_b[k] * gathered(cparts, k + 1, 128) * c_mask)
    _loop(0, 12, back_second, 2)
    clear(grad_b3, 2, 12)

    def b_own(k):
        pad_b[k] = (grad_b3[k + 2, 128:256, :].astype(F32) * own_c).astype(BF)
    _loop(0, 8, b_own, 4)

    def b_window(k):
        return jnp.concatenate([coarse3[k + 2], coarse3[k + 3], coarse3[k + 4]], axis=0)
    early_src[pl.ds(56, 36)] = jnp.zeros((36, 16, 128), F32)
    early_src[pl.ds(92, 4)] = jnp.zeros((4, 16, 128), F32)

    def b_step(j):
        early_src[pl.ds(56, 36)] += _dot_t(
            pair(b_window, j), pair(lambda k: pad_b[k], j)).reshape(36, 16, 128)
    _loop(0, 4, b_step, 2)
    early.pair()

    def back_third(k):
        cparts[k, 0:192] = _dot(wbt[...], grad_b3[k])
    _loop(0, 12, back_third, 6)

    def back_third_sum(k):
        grad_pool[k] = gathered(cparts, k + 1, 64).astype(BF)
    _loop(0, 10, back_third_sum, 5)
    _loop(0, 10, spread_step(grad_pool), 5)

    def back_join(k, s):
        at = slice(256 * s, 256 * s + 256)
        grad = grad_joined[k + 2, :, at].astype(F32) + 0.25 * up[k]
        grad_a3[2 * k - 1 + s] = _taps(slope_a[k, :, at] * grad * f_mask)[:, 0:128]
    early.plane()
    back_join(0, 1)

    def back_join_step(k):
        back_join(k, 0)
        back_join(k, 1)
    _loop(1, 9, back_join_step, 2)
    back_join(9, 0)
    clear(grad_a3, 1, 18)
    early.along_near()
    framed(pad_a, 1, 16, lambda h: grad_a3[h, 64:128, :])
    late_src[pl.ds(20, 12)] = jnp.zeros((12, 16, 128), F32)
    fine_weight_grad(pad_a, lambda i: x3[i + 6, :, 0:128], late_src, 0)
    late.pair()
    early.along_far()
    out_parts(wat, grad_a3)
    late.plane()
    out_rows(input_grad_ref)
    late.along_near()
    early.back_plane()
    late.along_far()
    early.back_pair()
    late.back_plane()
    early.finish()
    early_out[...] = early.whole[...]
    late.back_pair()
    late.finish()
    late_out[...] = late.whole[...]
    for copy in rim:
        copy.wait_send()


def _sum_scratch(tiles):
    half, chunk = tiles // 2, tiles // 32
    buffers = [
        ((tiles, 16, 128), BF), ((tiles, 16, 128), F32),
        ((half, 16, 128), BF), ((half, 16, 128), BF), ((half, 16, 128), BF),
        ((16, chunk, 16, 128), BF), ((4, chunk, 16, 128), F32), ((4, chunk, 16, 128), F32),
    ]
    sems = [pltpu.SemaphoreType.DMA((count,)) for count in (4, 4, 16, 16, 4, 4, 4, 4, 16, 16, 4, 4)]
    return [pltpu.VMEM(shape, dtype) for shape, dtype in buffers] + sems


def levels(level_input, cotangent, ka, kb, kc, kd):
    scratch = [
        ((64, 16, 128), BF), ((64, 16, 128), BF),
        ((9, 64, 64), BF), ((9, 64, 128), BF), ((9, 64, 128), BF), ((9, 64, 64), BF),
        ((16, 128, 128), BF), ((128, 128), BF), ((128, 128), BF),
        ((REACH, 128, 128), BF), ((REACH, 128, 128), BF), ((128, 128), BF), ((128, 128), BF),
        ((128, 128), BF), ((128, 128), BF), ((128, 128), BF), ((128, 128), BF),
        ((192, 192), BF), ((192, 192), BF), ((384, 192), BF), ((192, 384), BF),
        ((192, 384), BF), ((384, 192), BF), ((192, 192), BF), ((192, 192), BF),
        ((512, 128), BF), ((128, 256), BF),
        ((30, 192, 256), BF), ((30, 192, 256), BF), ((30, 192, 256), F32), ((30, 192, 256), F32),
        ((14, 384, 128), F32),
        ((14, 64, 512), BF), ((10, 64, 512), F32), ((12, 128, 128), F32),
        ((14, 192, 128), BF), ((12, 384, 128), BF), ((10, 64, 128), BF),
        ((18, 192, 128), BF), ((14, 64, 512), BF), ((14, 192, 128), BF), ((12, 384, 128), BF),
        ((10, 64, 128), BF), ((10, 64, 256), F32), ((18, 192, 128), BF),
        ((20, 64, 128), BF), ((8, 128, 128), BF), ((12, 64, 128), BF), ((20, 64, 128), BF),
        ((1024, 128), F32), ((192, 512), F32),
    ]
    dma = pltpu.SemaphoreType.DMA
    out = lambda shape, dtype: jax.ShapeDtypeStruct(shape, dtype)
    return pl.pallas_call(
        _levels_kernel,
        out_shape=(
            out((64, 16, 128), BF), out((64, 16, 128), BF), out((96, 16, 128), BF), out((32, 16, 128), BF)),
        in_specs=[pl.BlockSpec(memory_space=pltpu.HBM)] * 6,
        out_specs=(VMEM,) * 4,
        scratch_shapes=[pltpu.VMEM(shape, dtype) for shape, dtype in scratch]
        + [dma((6,)), dma((6,)), dma((6,))] + _sum_scratch(96) + _sum_scratch(32),
        compiler_params=pltpu.CompilerParams(
            collective_id=0, has_side_effects=True, vmem_limit_bytes=60 * 1024 * 1024),
        cost_estimate=pl.CostEstimate(flops=2000000000, bytes_accessed=8000000, transcendentals=1000000),
    )(level_input, cotangent, ka, kb, kc, kd)


def _finish_kernel(fine_scale, coarse_scale, result_in, input_grad_in, early_ref, late_ref,
                   result_ref, input_grad_ref, grad_a_ref, grad_b_ref, grad_c_ref, grad_d_ref):
    result_ref[...] = result_in[...]
    input_grad_ref[...] = input_grad_in[...]
    grad_c_ref[...] = early_ref[pl.ds(0, 36)].astype(F32).reshape(9, 64, 128) * coarse_scale
    grad_b_ref[...] = early_ref[pl.ds(56, 36)].astype(F32).reshape(9, 64, 128) * coarse_scale
    for ref, taps in ((grad_d_ref, early_ref[pl.ds(36, 20)]), (grad_a_ref, late_ref[pl.ds(0, 20)])):
        fine = taps.astype(F32).reshape(5, 64, 128) * fine_scale
        ref[pl.ds(0, 5)] = fine[:, :, 0:64]
        ref[pl.ds(5, 4)] = fine[0:4, :, 64:128]


def finish(result, input_grad, early, late, fine_scale, coarse_scale):
    out = lambda shape, dtype: jax.ShapeDtypeStruct(shape, dtype)
    return pl.pallas_call(
        functools.partial(_finish_kernel, fine_scale, coarse_scale),
        out_shape=(
            out((64, 16, 128), BF), out((64, 16, 128), BF), out((9, 64, 64), F32),
            out((9, 64, 128), F32), out((9, 64, 128), F32), out((9, 64, 64), F32)),
        in_specs=[VMEM] * 4,
        out_specs=(VMEM,) * 6,
        compiler_params=pltpu.CompilerParams(vmem_limit_bytes=8 * 1024 * 1024),
        cost_estimate=pl.CostEstimate(flops=1000000, bytes_accessed=2000000, transcendentals=0),
    )(result, input_grad, early, late)


def tap_major(kernel, order):
    taps = jnp.transpose(kernel, (2, 3) + order)
    return taps.reshape((9,) + taps.shape[2:])


def from_taps(grad, order):
    return jnp.transpose(grad.reshape((3, 3) + grad.shape[1:]), order)


def body(level_input, kernel_a, kernel_b, kernel_c, kernel_d, cotangent):
    total_cells = (
        level_input.shape[1] * level_input.shape[2] * lax.axis_size("rows") * lax.axis_size("cols")
    )
    parts = levels(
        level_input, cotangent,
        tap_major(kernel_a, (0, 1)), tap_major(kernel_b, (1, 0)),
        tap_major(kernel_c, (0, 1)), tap_major(kernel_d, (0, 1)))
    result_field, input_grad, grad_a, grad_b, grad_c, grad_d = finish(
        *parts, 1.0 / math.sqrt(total_cells), 1.0 / math.sqrt(total_cells // 4))
    return (
        result_field,
        input_grad,
        from_taps(grad_a, (2, 3, 0, 1)),
        from_taps(grad_b, (3, 2, 0, 1)),
        from_taps(grad_c, (2, 3, 0, 1)),
        from_taps(grad_d, (2, 3, 0, 1)),
    )


def solution(mesh):
    placed = (P(None, "rows", "cols"), P(), P(), P(), P(), P(None, "rows", "cols"))
    return jax.shard_map(
        body,
        mesh=mesh,
        in_specs=placed,
        out_specs=(P(None, "rows", "cols"), P(None, "rows", "cols"), P(), P(), P(), P()),
        check_vma=False,
    )
```

```python
import functools
import math

import jax
import jax.numpy as jnp
from jax import lax
from jax.experimental import pallas as pl
from jax.experimental.pallas import tpu as pltpu
from jax.sharding import PartitionSpec as P

MESH = pl.DeviceIdType.MESH
BF, F32 = jnp.bfloat16, jnp.float32
VMEM = pl.BlockSpec(memory_space=pltpu.VMEM)
GELU_SCALE = 0.7978845608028654
GELU_CUBE = 0.044715
REACH = 7


def _gelu_parts(x):
    square = x * x
    bend = jnp.tanh(GELU_SCALE * (x + GELU_CUBE * (x * square)))
    half = 0.5 + 0.5 * bend
    slope = half + (0.5 * GELU_SCALE) * x * (1.0 - bend * bend) * (1.0 + (3.0 * GELU_CUBE) * square)
    return x * half, slope


def _taps(x):
    lanes = x.shape[1]
    return jnp.concatenate(
        [pltpu.roll(x, 1, axis=1).astype(BF), x.astype(BF), pltpu.roll(x, lanes - 1, axis=1).astype(BF)],
        axis=0)


def _dot(a, b):
    return jnp.dot(a, b, preferred_element_type=F32)


def _dot_t(a, b):
    return lax.dot_general(a, b, (((1,), (1,)), ((), ())), preferred_element_type=F32)


def _loop(first, last, step, unroll=1):
    def body(i, carry):
        step(i)
        return carry
    lax.fori_loop(first, last, body, 0, unroll=unroll)


class _Sum:
    def __init__(self, whole, src, *rest):
        self.whole, self.src, self.sems = whole, src, rest[6:]
        (self.pair_out, self.pair_in, self.plane_out, self.plane_in, self.near_all, self.far_all) = rest[:6]
        self.half = src.shape[0] // 2
        self.piece, self.chunk = self.half // 4, self.half // 16
        rows, cols = lax.axis_index("rows"), lax.axis_index("cols")
        self.y, self.near, self.core = rows // 8, (rows // 2) % 4, rows % 2
        self.far_at, self.x = cols // 4, cols % 4
        self.partner = self.place(1 - self.core, 0, 0, 0, 0)
        self.steps = [(dy, dx) for dy in (2, 1, 3, 0) for dx in (2, 1, 3, 0)]
        self.base = self.core * self.half + self.y * self.piece + self.x * self.chunk
        self.started = []

    def place(self, core, dy, dx, dn, df):
        return (((self.y + dy) % 4) * 8 + ((self.near + dn) % 4) * 2 + core,
                ((self.far_at + df) % 4) * 4 + (self.x + dx) % 4)

    def peers(self):
        found = [self.partner]
        found += [self.place(self.core, dy, dx, 0, 0) for dy, dx in self.steps if (dy, dx) != (0, 0)]
        found += [self.place(self.core, 0, 0, d, 0) for d in (1, 2, 3)]
        found += [self.place(self.core, 0, 0, 0, d) for d in (1, 2, 3)]
        return found

    def send(self, src, dst, phase, k, peer):
        copy = pltpu.make_async_remote_copy(
            src_ref=src, dst_ref=dst, send_sem=self.sems[2 * phase].at[k],
            recv_sem=self.sems[2 * phase + 1].at[k], device_id=peer, device_id_type=MESH)
        copy.start()
        self.started.append(copy)
        return copy

    def pair(self):
        self.copies = {}
        theirs = (1 - self.core) * self.half
        for dy in (2, 1, 3, 0):
            first = ((self.y + dy) % 4) * self.piece
            piece = pl.ds(first, self.piece)
            self.pair_out[piece] = self.src[pl.ds(theirs + first, self.piece)].astype(BF)
            self.copies[dy] = self.send(
                self.pair_out.at[piece], self.pair_in.at[piece], 0, dy, self.partner)

    def plane(self):
        mine, pair, self.copies = self.core * self.half, self.copies, {}
        for dy, dx in self.steps:
            if dx == 2:
                pair[dy].wait_recv()
            first = ((self.y + dy) % 4) * self.piece + ((self.x + dx) % 4) * self.chunk
            chunk = pl.ds(first, self.chunk)
            both = self.src[pl.ds(mine + first, self.chunk)] + self.pair_in[chunk].astype(F32)
            if (dy, dx) == (0, 0):
                self.own = both
            else:
                k = dy * 4 + dx
                self.plane_out[chunk] = both.astype(BF)
                self.copies[k] = self.send(
                    self.plane_out.at[chunk], self.plane_in.at[k], 1, k,
                    self.place(self.core, dy, dx, 0, 0))

    def along_near(self):
        total = self.own
        for k in (4, 12, 1, 3, 8, 2, 5, 7, 13, 15, 6, 14, 9, 11, 10):
            self.copies[k].wait_recv()
            total = total + self.plane_in[k].astype(F32)
        self.near_all[self.near] = total
        at = self.near_all.at[self.near]
        self.copies = {}
        for d in (2, 1, 3):
            self.copies[d] = self.send(at, at, 2, d, self.place(self.core, 0, 0, d, 0))

    def along_far(self):
        for d in (1, 3, 2):
            self.copies[d].wait_recv()
        near = self.near_all
        self.far_all[self.far_at] = ((near[0] + near[1]) + near[2]) + near[3]
        at = self.far_all.at[self.far_at]
        self.copies = {}
        for d in (2, 1, 3):
            self.copies[d] = self.send(at, at, 3, d, self.place(self.core, 0, 0, 0, d))

    def back_plane(self):
        for d in (1, 3, 2):
            self.copies[d].wait_recv()
        far, chunk = self.far_all, pl.ds(self.base, self.chunk)
        self.whole[chunk] = (((far[0] + far[1]) + far[2]) + far[3]).astype(BF)
        at = self.whole.at[chunk]
        self.copies = {}
        for dy, dx in self.steps:
            if (dy, dx) != (0, 0):
                k = dy * 4 + dx
                self.copies[k] = self.send(at, at, 4, k, self.place(self.core, dy, dx, 0, 0))

    def back_pair(self):
        plane, self.copies = self.copies, {}
        for dy in (0, 1, 3, 2):
            for dx in (0, 1, 3, 2):
                if (dy, dx) != (0, 0):
                    plane[dy * 4 + dx].wait_recv()
            first = self.core * self.half + ((self.y - dy + 4) % 4) * self.piece
            at = self.whole.at[pl.ds(first, self.piece)]
            self.copies[dy] = self.send(at, at, 5, dy, self.partner)

    def finish(self):
        for dy in (0, 1, 3, 2):
            self.copies[dy].wait_recv()
        for copy in self.started:
            copy.wait_send()


def _levels_kernel(x_at, cot_at, ka_at, kb_at, kc_at, kd_at,
                   result_out, input_grad_out, early_out, late_out,
                   result_ref, input_grad_ref, x_ref, cot_ref, ka_ref, kb_ref, kc_ref, kd_ref,
                   rows_ref, left_ref, right_ref, above_ref, below_ref, from_left_ref, from_right_ref,
                   up_corners, down_corners, above_corners, below_corners,
                   wa, wat, wb, wbt, wc, wct, wd, wdt, pool, spread,
                   x3, cot3, parts, cot_parts, cparts, hidden, slope_a, slope_b, coarse3, middle3,
                   coarse_out, joined3, grad_joined, grad_coarse3, grad_b3, grad_pool, up, grad_a3,
                   pad_a, pad_b, pad_c, pad_d, flat, acc, *rest):
    load_sem, store_sem, rim_send, rim_recv = rest[:4]
    early_rest, late_rest = rest[4:24], rest[24:44]
    row, col = lax.axis_index("rows"), lax.axis_index("cols")
    height, width = lax.axis_size("rows"), lax.axis_size("cols")
    top = (row == 0).astype(jnp.int32)
    bottom = (row == height - 1).astype(jnp.int32)
    low = (col == 0).astype(jnp.int32)
    high = (col == width - 1).astype(jnp.int32)

    early, late = _Sum(*early_rest), _Sum(*late_rest)
    early_src, late_src = early.src, late.src

    def beside(dr, dc):
        return ((row + dr + height) % height, (col + dc + width) % width)

    around = [(0, -1), (0, 1), (-1, 0), (1, 0)]
    greeted = [beside(dr, dc) for dr, dc in around] + early.peers()
    barrier = pltpu.get_barrier_semaphore()
    for peer in greeted:
        pl.semaphore_signal(barrier, inc=1, device_id=peer, device_id_type=MESH)
    loads = [
        pltpu.make_async_copy(src, dst, load_sem.at[k]) for k, (src, dst) in enumerate((
            (x_at, x_ref), (cot_at, cot_ref), (ka_at, ka_ref), (kb_at, kb_ref), (kc_at, kc_ref), (kd_at, kd_ref)))]
    for load in loads:
        load.start()

    lane = lax.broadcasted_iota(jnp.int32, (64, 128), 1) // 8
    for field, ref in ((0, x_ref), (1, cot_ref)):
        loads[field].wait()
        flat[...] = ref[...].astype(F32).reshape(1024, 128)
        at = pl.ds(field * 64, 64)
        left = jnp.zeros((64, 128), F32)
        right = jnp.zeros((64, 128), F32)
        for h in range(16):
            line = flat[pl.ds(h, 64, stride=16), :]
            rows_ref[h, at, :] = line.astype(BF)
            left = jnp.where(lane == h, line if h == 0 else pltpu.roll(line, 8 * h, axis=1), left)
            right = jnp.where(lane == h, line if h == 15 else pltpu.roll(line, 8 * h + 8, axis=1), right)
        left_ref[at, :] = left.astype(BF)
        right_ref[at, :] = right.astype(BF)
    pl.semaphore_wait(barrier, len(greeted))
    rim = []

    def push(src, dst, offset):
        rim.append(pltpu.make_async_remote_copy(
            src_ref=src, dst_ref=dst, send_sem=rim_send.at[len(rim)], recv_sem=rim_recv.at[len(rim)],
            device_id=beside(*offset), device_id_type=MESH))
        rim[-1].start()

    push(left_ref, from_right_ref, (0, -1))
    push(right_ref, from_left_ref, (0, 1))
    push(rows_ref.at[pl.ds(0, REACH)], below_ref, (-1, 0))
    push(rows_ref.at[pl.ds(16 - REACH, REACH)], above_ref, (1, 0))
    f_lane = lax.broadcasted_iota(jnp.int32, (1, 256), 1)
    c_lane = lax.broadcasted_iota(jnp.int32, (1, 128), 1)
    f_mask = ((f_lane < 136 - 8 * high) | (f_lane >= 248 + 8 * low)).astype(F32)
    c_mask = ((c_lane < 68 - 4 * high) | (c_lane >= 124 + 4 * low)).astype(F32)
    own_c = (c_lane < 64).astype(F32)

    for load in loads[2:]:
        load.wait()
    for a in range(3):
        for b in range(3):
            tap, flip = 3 * a + b, 8 - (3 * a + b)
            at64, at128 = pl.ds(64 * a, 64), pl.ds(128 * a, 128)
            col64, col128 = slice(64 * b, 64 * b + 64), slice(128 * b, 128 * b + 128)
            wa[at64, col64] = ka_ref[tap]
            wd[at64, col64] = kd_ref[tap]
            wc[at64, col128] = kc_ref[tap]
            wbt[at64, col128] = kb_ref[flip]
            wat[at64, col64] = ka_ref[flip].astype(F32).T.astype(BF)
            wdt[at64, col64] = kd_ref[flip].astype(F32).T.astype(BF)
            wb[at128, col64] = kb_ref[tap].astype(F32).T.astype(BF)
            wct[at128, col64] = kc_ref[flip].astype(F32).T.astype(BF)
    cell = lax.broadcasted_iota(jnp.int32, (512, 128), 0)
    block = lax.broadcasted_iota(jnp.int32, (512, 128), 1)
    pool[...] = ((cell % 256) // 2 == block).astype(F32).astype(BF)
    cell = lax.broadcasted_iota(jnp.int32, (128, 256), 1)
    block = lax.broadcasted_iota(jnp.int32, (128, 256), 0)
    spread[...] = (cell // 2 == block).astype(F32).astype(BF)

    side_lane = lax.broadcasted_iota(jnp.int32, (128, 128), 1)

    def unpack(i):
        h = i - REACH
        if h < 0:
            center, left, right, p = above_ref[h + REACH], above_corners[...], above_corners[...], h + 16
            turn_left, turn_right = (184 - 8 * p) % 128, 128 - 8 * p
        elif h < 16:
            center, left, right, p = rows_ref[h], from_left_ref[...], from_right_ref[...], h
            turn_left, turn_right = 120 - 8 * p, (128 - 8 * p) % 128
        else:
            center, left, right, p = below_ref[h - 16], below_corners[...], below_corners[...], h - 16
            turn_left, turn_right = 120 - 8 * p, 64 - 8 * p
        left, right = left.astype(F32), right.astype(F32)
        right = pltpu.roll(right, turn_right, axis=1) if turn_right else right
        left = pltpu.roll(left, turn_left, axis=1) if turn_left else left
        side = jnp.where(side_lane < 8, right, left)
        wide = jnp.concatenate([center.astype(F32), side], axis=1) * f_mask
        x3[i] = _taps(wide[:64])
        cot3[i] = _taps(wide[64:])

    def conv(weights, source, into, first, last, unroll):
        def step(i):
            into[i] = _dot(weights[...], source[i])
        _loop(first, last, step, unroll)

    rim[0].wait_recv()
    rim[1].wait_recv()
    left, right = from_left_ref[...].astype(F32), from_right_ref[...].astype(F32)
    up_corners[...] = jnp.where(side_lane < 64, left, pltpu.roll(right, 64, axis=1)).astype(BF)
    down_corners[...] = jnp.where(side_lane < 64, pltpu.roll(left, 64, axis=1), right).astype(BF)
    push(up_corners, below_corners, (-1, 0))
    push(down_corners, above_corners, (1, 0))
    for i in range(REACH, REACH + 16):
        unpack(i)
    conv(wa, x3, parts, 7, 23, 8)
    conv(wdt, cot3, cot_parts, 7, 23, 8)
    for copy in rim[2:]:
        copy.wait_recv()
    for i in list(range(REACH)) + list(range(REACH + 16, 30)):
        unpack(i)

    def clear(ref, top_rows, total):
        @pl.when(top == 1)
        def _():
            ref[pl.ds(0, top_rows)] = jnp.zeros((top_rows,) + ref.shape[1:], ref.dtype)

        @pl.when(bottom == 1)
        def _():
            ref[pl.ds(total - top_rows, top_rows)] = jnp.zeros((top_rows,) + ref.shape[1:], ref.dtype)

    clear(x3, 7, 30)
    clear(cot3, 7, 30)

    def gathered(from_, i, outs):
        return from_[i - 1, 0:outs] + from_[i, outs:2 * outs] + from_[i + 1, 2 * outs:3 * outs]

    for first_row in (0, 23):
        conv(wa, x3, parts, first_row, first_row + 7, 7)
        conv(wdt, cot3, cot_parts, first_row, first_row + 7, 7)

    def first(with_slope):
        def step(k):
            for s in range(2):
                pre = gathered(parts, 2 * k + 1 + s, 64)
                value, slope = _gelu_parts(pre)
                hidden[k, :, 256 * s:256 * s + 256] = (value * f_mask).astype(BF)
                if with_slope:
                    slope_a[k - 2, :, 256 * s:256 * s + 256] = slope
        return step
    _loop(0, 2, first(False), 2)
    _loop(2, 12, first(True), 5)
    _loop(12, 14, first(False), 2)
    clear(hidden, 3, 14)

    def pool_step(k):
        coarse3[k] = _taps((_dot(hidden[k], pool[...]) * 0.25).astype(BF).astype(F32))
    _loop(0, 14, pool_step, 14)

    conv(wb, coarse3, cparts, 0, 14, 7)

    def second(k):
        value, slope = _gelu_parts(gathered(cparts, k + 1, 128))
        middle3[k] = _taps(value * c_mask)
        slope_b[k] = slope
    _loop(0, 12, second, 6)
    clear(middle3, 2, 12)

    def third(k):
        cparts[k, 0:192] = _dot(wc[...], middle3[k])
    _loop(0, 12, third, 12)

    def third_sum(k):
        coarse_out[k] = (gathered(cparts, k + 1, 64) * c_mask).astype(BF)
    _loop(0, 10, third_sum, 10)
    clear(coarse_out, 1, 10)

    def spread_step(source):
        def step(k):
            up[k] = _dot(source[k], spread[...])
        return step
    _loop(0, 10, spread_step(coarse_out), 10)

    def join(k, s):
        both = hidden[k + 2, :, 256 * s:256 * s + 256].astype(F32) + up[k]
        joined3[2 * k - 1 + s] = _taps(both)[:, 0:128]
    join(0, 1)

    def join_step(k):
        join(k, 0)
        join(k, 1)
    _loop(1, 9, join_step, 4)
    join(9, 0)

    def out_parts(weights, source):
        def step(i):
            parts[i, :, 0:128] = _dot(weights[...], source[i])
        _loop(0, 18, step, 9)

    def out_rows(ref):
        for h in range(16):
            flat[pl.ds(h, 64, stride=16), :] = gathered(
                parts.at[:, :, pl.ds(0, 128)], h + 1, 64)
        ref[...] = flat[...].reshape(64, 16, 128).astype(BF)


    def stacked(pad, j):
        return jnp.concatenate([pad[j + 2], pad[j + 1], pad[j]], axis=0)

    def pair(one, j):
        return jnp.concatenate([one(2 * j), one(2 * j + 1)], axis=1)

    def framed(pad, first, count, own):
        pad[pl.ds(0, 2)] = jnp.zeros((2,) + pad.shape[1:], BF)
        pad[pl.ds(count + 2, 2)] = jnp.zeros((2,) + pad.shape[1:], BF)

        def step(h):
            pad[h + 2] = own(h + first)
        _loop(0, count, step, 4)

    def fine_weight_grad(pad, window, src, first):
        acc[0:192, 0:192] = jnp.zeros((192, 192), F32)

        def step(j):
            acc[0:192, 0:192] += _dot_t(pair(lambda i: stacked(pad, i), j), pair(window, j))
        _loop(0, 9, step, 9)

        def tap(t):
            if t > 8:
                return jnp.zeros((64, 64), F32)
            a, b = t // 3, t % 3
            return acc[64 * a:64 * a + 64, 64 * b:64 * b + 64]
        for t in range(5):
            both = jnp.concatenate([tap(t), tap(t + 5)], axis=1)
            src[pl.ds(first + 4 * t, 4)] = both.reshape(4, 16, 128)

    framed(pad_d, 7, 16, lambda h: cot3[h, 64:128, 0:128])
    fine_weight_grad(pad_d, lambda i: joined3[i], early_src, 36)


    def back_first(k):
        for s in range(2):
            grad = gathered(cot_parts, 2 * k + 1 + s, 64) * f_mask
            grad_joined[k, :, 256 * s:256 * s + 256] = grad.astype(BF)
    _loop(0, 14, back_first, 7)
    clear(grad_joined, 3, 14)

    def back_pool(k):
        grad_coarse3[k] = _taps(_dot(grad_joined[k], pool[...]).astype(BF).astype(F32))
    _loop(0, 14, back_pool, 14)

    framed(pad_c, 3, 8, lambda k: (grad_coarse3[k, 64:128, :].astype(F32) * own_c).astype(BF))
    acc[0:192, 0:384] = jnp.zeros((192, 384), F32)

    def c_step(j):
        acc[0:192, 0:384] += _dot_t(
            pair(lambda i: stacked(pad_c, i), j), pair(lambda i: middle3[i + 1], j))
    _loop(0, 5, c_step, 5)
    for a in range(3):
        for b in range(3):
            early_src[pl.ds(4 * (3 * a + b), 4)] = acc[
                64 * a:64 * a + 64, 128 * b:128 * b + 128].reshape(4, 16, 128)
    conv(wct, grad_coarse3, cparts, 0, 14, 7)

    def back_second(k):
        grad_b3[k] = _taps(slope_b[k] * gathered(cparts, k + 1, 128) * c_mask)
    _loop(0, 12, back_second, 6)
    clear(grad_b3, 2, 12)

    def b_own(k):
        pad_b[k] = (grad_b3[k + 2, 128:256, :].astype(F32) * own_c).astype(BF)
    _loop(0, 8, b_own, 4)

    def b_window(k):
        return jnp.concatenate([coarse3[k + 2], coarse3[k + 3], coarse3[k + 4]], axis=0)
    early_src[pl.ds(56, 36)] = jnp.zeros((36, 16, 128), F32)
    early_src[pl.ds(92, 4)] = jnp.zeros((4, 16, 128), F32)

    def b_step(j):
        early_src[pl.ds(56, 36)] += _dot_t(
            pair(b_window, j), pair(lambda k: pad_b[k], j)).reshape(36, 16, 128)
    _loop(0, 4, b_step, 4)
    early.pair()

    def back_third(k):
        cparts[k, 0:192] = _dot(wbt[...], grad_b3[k])
    _loop(0, 12, back_third, 12)

    def back_third_sum(k):
        grad_pool[k] = gathered(cparts, k + 1, 64).astype(BF)
    _loop(0, 10, back_third_sum, 10)
    _loop(0, 10, spread_step(grad_pool), 10)

    def back_join(k, s):
        at = slice(256 * s, 256 * s + 256)
        grad = grad_joined[k + 2, :, at].astype(F32) + 0.25 * up[k]
        grad_a3[2 * k - 1 + s] = _taps(slope_a[k, :, at] * grad * f_mask)[:, 0:128]
    early.plane()
    back_join(0, 1)

    def back_join_step(k):
        back_join(k, 0)
        back_join(k, 1)
    _loop(1, 9, back_join_step, 4)
    back_join(9, 0)
    clear(grad_a3, 1, 18)
    early.along_near()
    framed(pad_a, 1, 16, lambda h: grad_a3[h, 64:128, :])
    late_src[pl.ds(20, 12)] = jnp.zeros((12, 16, 128), F32)
    fine_weight_grad(pad_a, lambda i: x3[i + 6, :, 0:128], late_src, 0)
    stores = []

    def store(src, dst):
        stores.append(pltpu.make_async_copy(src, dst, store_sem.at[len(stores)]))
        stores[-1].start()

    late.pair()
    early.along_far()
    out_parts(wd, joined3)
    late.plane()
    out_rows(result_ref)
    store(result_ref, result_out)
    out_parts(wat, grad_a3)
    late.along_near()
    early.back_plane()
    out_rows(input_grad_ref)
    store(input_grad_ref, input_grad_out)
    late.along_far()
    early.back_pair()
    late.back_plane()
    early.finish()
    store(early.whole, early_out)
    late.back_pair()
    late.finish()
    store(late.whole, late_out)
    for copy in rim:
        copy.wait_send()
    for copy in stores:
        copy.wait()


def _sum_scratch(tiles):
    half, chunk = tiles // 2, tiles // 32
    buffers = [
        ((tiles, 16, 128), BF), ((tiles, 16, 128), F32),
        ((half, 16, 128), BF), ((half, 16, 128), BF), ((half, 16, 128), BF),
        ((16, chunk, 16, 128), BF), ((4, chunk, 16, 128), F32), ((4, chunk, 16, 128), F32),
    ]
    sems = [pltpu.SemaphoreType.DMA((count,)) for count in (4, 4, 16, 16, 4, 4, 4, 4, 16, 16, 4, 4)]
    return [pltpu.VMEM(shape, dtype) for shape, dtype in buffers] + sems


def levels(level_input, cotangent, ka, kb, kc, kd):
    scratch = [
        ((64, 16, 128), BF), ((64, 16, 128), BF), ((64, 16, 128), BF), ((64, 16, 128), BF),
        ((9, 64, 64), BF), ((9, 64, 128), BF), ((9, 64, 128), BF), ((9, 64, 64), BF),
        ((16, 128, 128), BF), ((128, 128), BF), ((128, 128), BF),
        ((REACH, 128, 128), BF), ((REACH, 128, 128), BF), ((128, 128), BF), ((128, 128), BF),
        ((128, 128), BF), ((128, 128), BF), ((128, 128), BF), ((128, 128), BF),
        ((192, 192), BF), ((192, 192), BF), ((384, 192), BF), ((192, 384), BF),
        ((192, 384), BF), ((384, 192), BF), ((192, 192), BF), ((192, 192), BF),
        ((512, 128), BF), ((128, 256), BF),
        ((30, 192, 256), BF), ((30, 192, 256), BF), ((30, 192, 256), F32), ((30, 192, 256), F32),
        ((14, 384, 128), F32),
        ((14, 64, 512), BF), ((10, 64, 512), F32), ((12, 128, 128), F32),
        ((14, 192, 128), BF), ((12, 384, 128), BF), ((10, 64, 128), BF),
        ((18, 192, 128), BF), ((14, 64, 512), BF), ((14, 192, 128), BF), ((12, 384, 128), BF),
        ((10, 64, 128), BF), ((10, 64, 256), F32), ((18, 192, 128), BF),
        ((20, 64, 128), BF), ((8, 128, 128), BF), ((12, 64, 128), BF), ((20, 64, 128), BF),
        ((1024, 128), F32), ((192, 512), F32),
    ]
    dma = pltpu.SemaphoreType.DMA
    out = lambda shape, dtype: jax.ShapeDtypeStruct(shape, dtype)
    return pl.pallas_call(
        _levels_kernel,
        out_shape=(
            out((64, 16, 128), BF), out((64, 16, 128), BF), out((96, 16, 128), BF), out((32, 16, 128), BF)),
        in_specs=[pl.BlockSpec(memory_space=pltpu.HBM)] * 6,
        out_specs=(pl.BlockSpec(memory_space=pltpu.HBM),) * 4,
        scratch_shapes=[pltpu.VMEM(shape, dtype) for shape, dtype in scratch]
        + [dma((6,)), dma((4,)), dma((6,)), dma((6,))] + _sum_scratch(96) + _sum_scratch(32),
        compiler_params=pltpu.CompilerParams(
            collective_id=0, has_side_effects=True, vmem_limit_bytes=60 * 1024 * 1024),
        cost_estimate=pl.CostEstimate(flops=2000000000, bytes_accessed=8000000, transcendentals=1000000),
    )(level_input, cotangent, ka, kb, kc, kd)


def _finish_kernel(fine_scale, coarse_scale, result_in, input_grad_in, early_ref, late_ref,
                   result_ref, input_grad_ref, grad_a_ref, grad_b_ref, grad_c_ref, grad_d_ref):
    result_ref[...] = result_in[...]
    input_grad_ref[...] = input_grad_in[...]
    grad_c_ref[...] = early_ref[pl.ds(0, 36)].astype(F32).reshape(9, 64, 128) * coarse_scale
    grad_b_ref[...] = early_ref[pl.ds(56, 36)].astype(F32).reshape(9, 64, 128) * coarse_scale
    for ref, taps in ((grad_d_ref, early_ref[pl.ds(36, 20)]), (grad_a_ref, late_ref[pl.ds(0, 20)])):
        fine = taps.astype(F32).reshape(5, 64, 128) * fine_scale
        ref[pl.ds(0, 5)] = fine[:, :, 0:64]
        ref[pl.ds(5, 4)] = fine[0:4, :, 64:128]


def finish(result, input_grad, early, late, fine_scale, coarse_scale):
    out = lambda shape, dtype: jax.ShapeDtypeStruct(shape, dtype)
    return pl.pallas_call(
        functools.partial(_finish_kernel, fine_scale, coarse_scale),
        out_shape=(
            out((64, 16, 128), BF), out((64, 16, 128), BF), out((9, 64, 64), F32),
            out((9, 64, 128), F32), out((9, 64, 128), F32), out((9, 64, 64), F32)),
        in_specs=[VMEM] * 4,
        out_specs=(VMEM,) * 6,
        compiler_params=pltpu.CompilerParams(vmem_limit_bytes=60 * 1024 * 1024),
        cost_estimate=pl.CostEstimate(flops=1000000, bytes_accessed=2000000, transcendentals=0),
    )(result, input_grad, early, late)


def tap_major(kernel, order):
    taps = jnp.transpose(kernel, (2, 3) + order)
    return taps.reshape((9,) + taps.shape[2:])


def from_taps(grad, order):
    return jnp.transpose(grad.reshape((3, 3) + grad.shape[1:]), order)


def body(level_input, kernel_a, kernel_b, kernel_c, kernel_d, cotangent):
    total_cells = (
        level_input.shape[1] * level_input.shape[2] * lax.axis_size("rows") * lax.axis_size("cols")
    )
    parts = levels(
        level_input, cotangent,
        tap_major(kernel_a, (0, 1)), tap_major(kernel_b, (1, 0)),
        tap_major(kernel_c, (0, 1)), tap_major(kernel_d, (0, 1)))
    result_field, input_grad, grad_a, grad_b, grad_c, grad_d = finish(
        *parts, 1.0 / math.sqrt(total_cells), 1.0 / math.sqrt(total_cells // 4))
    return (
        result_field,
        input_grad,
        from_taps(grad_a, (2, 3, 0, 1)),
        from_taps(grad_b, (3, 2, 0, 1)),
        from_taps(grad_c, (2, 3, 0, 1)),
        from_taps(grad_d, (2, 3, 0, 1)),
    )


def solution(mesh):
    placed = (P(None, "rows", "cols"), P(), P(), P(), P(), P(None, "rows", "cols"))
    return jax.shard_map(
        body,
        mesh=mesh,
        in_specs=placed,
        out_specs=(P(None, "rows", "cols"), P(None, "rows", "cols"), P(), P(), P(), P()),
        check_vma=False,
    )
```

```python
import functools
import math

import jax
import jax.numpy as jnp
from jax import lax
from jax.experimental import pallas as pl
from jax.experimental.pallas import tpu as pltpu
from jax.sharding import PartitionSpec as P

MESH = pl.DeviceIdType.MESH
BF, F32 = jnp.bfloat16, jnp.float32
VMEM = pl.BlockSpec(memory_space=pltpu.VMEM)
GELU_SCALE = 0.7978845608028654
GELU_CUBE = 0.044715
REACH = 7


def _gelu_parts(x):
    square = x * x
    bend = jnp.tanh(GELU_SCALE * (x + GELU_CUBE * (x * square)))
    half = 0.5 + 0.5 * bend
    slope = half + (0.5 * GELU_SCALE) * x * (1.0 - bend * bend) * (1.0 + (3.0 * GELU_CUBE) * square)
    return x * half, slope


def _taps(x):
    lanes = x.shape[1]
    return jnp.concatenate(
        [pltpu.roll(x, 1, axis=1).astype(BF), x.astype(BF), pltpu.roll(x, lanes - 1, axis=1).astype(BF)],
        axis=0)


def _dot(a, b):
    return jnp.dot(a, b, preferred_element_type=F32)


def _dot_t(a, b):
    return lax.dot_general(a, b, (((1,), (1,)), ((), ())), preferred_element_type=F32)


def _loop(first, last, step, unroll=1):
    def body(i, carry):
        step(i)
        return carry
    lax.fori_loop(first, last, body, 0, unroll=unroll)


class _Sum:
    def __init__(self, whole, src, *rest):
        self.whole, self.src, self.sems = whole, src, rest[6:]
        (self.pair_out, self.pair_in, self.plane_out, self.plane_in, self.near_all, self.far_all) = rest[:6]
        self.half = src.shape[0] // 2
        self.piece, self.chunk = self.half // 4, self.half // 16
        rows, cols = lax.axis_index("rows"), lax.axis_index("cols")
        self.y, self.near, self.core = rows // 8, (rows // 2) % 4, rows % 2
        self.far_at, self.x = cols // 4, cols % 4
        self.partner = self.place(1 - self.core, 0, 0, 0, 0)
        self.steps = [(dy, dx) for dy in (2, 1, 3, 0) for dx in (2, 1, 3, 0)]
        self.base = self.core * self.half + self.y * self.piece + self.x * self.chunk
        self.started = []

    def place(self, core, dy, dx, dn, df):
        return (((self.y + dy) % 4) * 8 + ((self.near + dn) % 4) * 2 + core,
                ((self.far_at + df) % 4) * 4 + (self.x + dx) % 4)

    def peers(self):
        found = [self.partner]
        found += [self.place(self.core, dy, dx, 0, 0) for dy, dx in self.steps if (dy, dx) != (0, 0)]
        found += [self.place(self.core, 0, 0, d, 0) for d in (1, 2, 3)]
        found += [self.place(self.core, 0, 0, 0, d) for d in (1, 2, 3)]
        return found

    def send(self, src, dst, phase, k, peer):
        copy = pltpu.make_async_remote_copy(
            src_ref=src, dst_ref=dst, send_sem=self.sems[2 * phase].at[k],
            recv_sem=self.sems[2 * phase + 1].at[k], device_id=peer, device_id_type=MESH)
        copy.start()
        self.started.append(copy)
        return copy

    def pair(self):
        self.copies = {}
        theirs = (1 - self.core) * self.half
        for dy in (2, 1, 3, 0):
            first = ((self.y + dy) % 4) * self.piece
            piece = pl.ds(first, self.piece)
            self.pair_out[piece] = self.src[pl.ds(theirs + first, self.piece)].astype(BF)
            self.copies[dy] = self.send(
                self.pair_out.at[piece], self.pair_in.at[piece], 0, dy, self.partner)

    def plane(self):
        mine, pair, self.copies = self.core * self.half, self.copies, {}
        for dy, dx in self.steps:
            if dx == 2:
                pair[dy].wait_recv()
            first = ((self.y + dy) % 4) * self.piece + ((self.x + dx) % 4) * self.chunk
            chunk = pl.ds(first, self.chunk)
            both = self.src[pl.ds(mine + first, self.chunk)] + self.pair_in[chunk].astype(F32)
            if (dy, dx) == (0, 0):
                self.own = both
            else:
                k = dy * 4 + dx
                self.plane_out[chunk] = both.astype(BF)
                self.copies[k] = self.send(
                    self.plane_out.at[chunk], self.plane_in.at[k], 1, k,
                    self.place(self.core, dy, dx, 0, 0))

    def along_near(self):
        total = self.own
        for k in (4, 12, 1, 3, 8, 2, 5, 7, 13, 15, 6, 14, 9, 11, 10):
            self.copies[k].wait_recv()
            total = total + self.plane_in[k].astype(F32)
        self.near_all[self.near] = total
        at = self.near_all.at[self.near]
        self.copies = {}
        for d in (2, 1, 3):
            self.copies[d] = self.send(at, at, 2, d, self.place(self.core, 0, 0, d, 0))

    def along_far(self):
        for d in (1, 3, 2):
            self.copies[d].wait_recv()
        near = self.near_all
        self.far_all[self.far_at] = ((near[0] + near[1]) + near[2]) + near[3]
        at = self.far_all.at[self.far_at]
        self.copies = {}
        for d in (2, 1, 3):
            self.copies[d] = self.send(at, at, 3, d, self.place(self.core, 0, 0, 0, d))

    def back_plane(self):
        for d in (1, 3, 2):
            self.copies[d].wait_recv()
        far, chunk = self.far_all, pl.ds(self.base, self.chunk)
        self.whole[chunk] = (((far[0] + far[1]) + far[2]) + far[3]).astype(BF)
        at = self.whole.at[chunk]
        self.copies = {}
        for dy, dx in self.steps:
            if (dy, dx) != (0, 0):
                k = dy * 4 + dx
                self.copies[k] = self.send(at, at, 4, k, self.place(self.core, dy, dx, 0, 0))

    def back_pair(self):
        plane, self.copies = self.copies, {}
        for dy in (0, 1, 3, 2):
            for dx in (0, 1, 3, 2):
                if (dy, dx) != (0, 0):
                    plane[dy * 4 + dx].wait_recv()
            first = self.core * self.half + ((self.y - dy + 4) % 4) * self.piece
            at = self.whole.at[pl.ds(first, self.piece)]
            self.copies[dy] = self.send(at, at, 5, dy, self.partner)

    def finish(self):
        for dy in (0, 1, 3, 2):
            self.copies[dy].wait_recv()
        for copy in self.started:
            copy.wait_send()


def _levels_kernel(x_at, cot_at, ka_at, kb_at, kc_at, kd_at,
                   result_out, input_grad_out, early_out, late_out,
                   result_ref, input_grad_ref, x_ref, cot_ref, ka_ref, kb_ref, kc_ref, kd_ref,
                   rows_ref, left_ref, right_ref, above_ref, below_ref, from_left_ref, from_right_ref,
                   up_corners, down_corners, above_corners, below_corners,
                   wa, wat, wb, wbt, wc, wct, wd, wdt, pool, spread,
                   x3, cot3, parts, cot_parts, cparts, hidden, slope_a, slope_b, coarse3, middle3,
                   coarse_out, joined3, grad_joined, grad_coarse3, grad_b3, grad_pool, up, grad_a3,
                   pad_a, pad_b, pad_c, pad_d, flat, acc, *rest):
    load_sem, store_sem, rim_send, rim_recv = rest[:4]
    early_rest, late_rest = rest[4:24], rest[24:44]
    row, col = lax.axis_index("rows"), lax.axis_index("cols")
    height, width = lax.axis_size("rows"), lax.axis_size("cols")
    top = (row == 0).astype(jnp.int32)
    bottom = (row == height - 1).astype(jnp.int32)
    low = (col == 0).astype(jnp.int32)
    high = (col == width - 1).astype(jnp.int32)

    early, late = _Sum(*early_rest), _Sum(*late_rest)
    early_src, late_src = early.src, late.src

    def beside(dr, dc):
        return ((row + dr + height) % height, (col + dc + width) % width)

    around = [(0, -1), (0, 1), (-1, 0), (1, 0)]
    greeted = [beside(dr, dc) for dr, dc in around] + early.peers()
    barrier = pltpu.get_barrier_semaphore()
    for peer in greeted:
        pl.semaphore_signal(barrier, inc=1, device_id=peer, device_id_type=MESH)
    loads = [
        pltpu.make_async_copy(src, dst, load_sem.at[k]) for k, (src, dst) in enumerate((
            (x_at, x_ref), (cot_at, cot_ref), (ka_at, ka_ref), (kb_at, kb_ref), (kc_at, kc_ref), (kd_at, kd_ref)))]
    for load in loads:
        load.start()

    lane = lax.broadcasted_iota(jnp.int32, (64, 128), 1) // 8
    for field, ref in ((0, x_ref), (1, cot_ref)):
        loads[field].wait()
        flat[...] = ref[...].astype(F32).reshape(1024, 128)
        at = pl.ds(field * 64, 64)
        left = jnp.zeros((64, 128), F32)
        right = jnp.zeros((64, 128), F32)
        for h in range(16):
            line = flat[pl.ds(h, 64, stride=16), :]
            rows_ref[h, at, :] = line.astype(BF)
            left = jnp.where(lane == h, line if h == 0 else pltpu.roll(line, 8 * h, axis=1), left)
            right = jnp.where(lane == h, line if h == 15 else pltpu.roll(line, 8 * h + 8, axis=1), right)
        left_ref[at, :] = left.astype(BF)
        right_ref[at, :] = right.astype(BF)
    pl.semaphore_wait(barrier, len(greeted))
    rim = []

    def push(src, dst, offset):
        rim.append(pltpu.make_async_remote_copy(
            src_ref=src, dst_ref=dst, send_sem=rim_send.at[len(rim)], recv_sem=rim_recv.at[len(rim)],
            device_id=beside(*offset), device_id_type=MESH))
        rim[-1].start()

    push(left_ref, from_right_ref, (0, -1))
    push(right_ref, from_left_ref, (0, 1))
    push(rows_ref.at[pl.ds(0, REACH)], below_ref, (-1, 0))
    push(rows_ref.at[pl.ds(16 - REACH, REACH)], above_ref, (1, 0))
    f_lane = lax.broadcasted_iota(jnp.int32, (1, 256), 1)
    c_lane = lax.broadcasted_iota(jnp.int32, (1, 128), 1)
    f_mask = ((f_lane < 136 - 8 * high) | (f_lane >= 248 + 8 * low)).astype(F32)
    c_mask = ((c_lane < 68 - 4 * high) | (c_lane >= 124 + 4 * low)).astype(F32)
    own_c = (c_lane < 64).astype(F32)

    for load in loads[2:]:
        load.wait()
    for a in range(3):
        for b in range(3):
            tap, flip = 3 * a + b, 8 - (3 * a + b)
            at64, at128 = pl.ds(64 * a, 64), pl.ds(128 * a, 128)
            col64, col128 = slice(64 * b, 64 * b + 64), slice(128 * b, 128 * b + 128)
            wa[at64, col64] = ka_ref[tap]
            wd[at64, col64] = kd_ref[tap]
            wc[at64, col128] = kc_ref[tap]
            wbt[at64, col128] = kb_ref[flip]
            wat[at64, col64] = ka_ref[flip].astype(F32).T.astype(BF)
            wdt[at64, col64] = kd_ref[flip].astype(F32).T.astype(BF)
            wb[at128, col64] = kb_ref[tap].astype(F32).T.astype(BF)
            wct[at128, col64] = kc_ref[flip].astype(F32).T.astype(BF)
    cell = lax.broadcasted_iota(jnp.int32, (512, 128), 0)
    block = lax.broadcasted_iota(jnp.int32, (512, 128), 1)
    pool[...] = ((cell % 256) // 2 == block).astype(F32).astype(BF)
    cell = lax.broadcasted_iota(jnp.int32, (128, 256), 1)
    block = lax.broadcasted_iota(jnp.int32, (128, 256), 0)
    spread[...] = (cell // 2 == block).astype(F32).astype(BF)

    side_lane = lax.broadcasted_iota(jnp.int32, (128, 128), 1)

    def unpack(i):
        h = i - REACH
        if h < 0:
            center, left, right, p = above_ref[h + REACH], above_corners[...], above_corners[...], h + 16
            turn_left, turn_right = (184 - 8 * p) % 128, 128 - 8 * p
        elif h < 16:
            center, left, right, p = rows_ref[h], from_left_ref[...], from_right_ref[...], h
            turn_left, turn_right = 120 - 8 * p, (128 - 8 * p) % 128
        else:
            center, left, right, p = below_ref[h - 16], below_corners[...], below_corners[...], h - 16
            turn_left, turn_right = 120 - 8 * p, 64 - 8 * p
        left, right = left.astype(F32), right.astype(F32)
        right = pltpu.roll(right, turn_right, axis=1) if turn_right else right
        left = pltpu.roll(left, turn_left, axis=1) if turn_left else left
        side = jnp.where(side_lane < 8, right, left)
        wide = jnp.concatenate([center.astype(F32), side], axis=1) * f_mask
        x3[i] = _taps(wide[:64])
        cot3[i] = _taps(wide[64:])

    def conv(weights, source, into, first, last, unroll):
        def step(i):
            into[i] = _dot(weights[...], source[i])
        _loop(first, last, step, unroll)

    rim[0].wait_recv()
    rim[1].wait_recv()
    left, right = from_left_ref[...].astype(F32), from_right_ref[...].astype(F32)
    up_corners[...] = jnp.where(side_lane < 64, left, pltpu.roll(right, 64, axis=1)).astype(BF)
    down_corners[...] = jnp.where(side_lane < 64, pltpu.roll(left, 64, axis=1), right).astype(BF)
    push(up_corners, below_corners, (-1, 0))
    push(down_corners, above_corners, (1, 0))
    for i in range(REACH, REACH + 16):
        unpack(i)
    conv(wa, x3, parts, 7, 23, 8)
    conv(wdt, cot3, cot_parts, 7, 23, 8)
    for copy in rim[2:]:
        copy.wait_recv()
    for i in list(range(REACH)) + list(range(REACH + 16, 30)):
        unpack(i)

    def clear(ref, top_rows, total):
        @pl.when(top == 1)
        def _():
            ref[pl.ds(0, top_rows)] = jnp.zeros((top_rows,) + ref.shape[1:], ref.dtype)

        @pl.when(bottom == 1)
        def _():
            ref[pl.ds(total - top_rows, top_rows)] = jnp.zeros((top_rows,) + ref.shape[1:], ref.dtype)

    clear(x3, 7, 30)
    clear(cot3, 7, 30)

    def gathered(from_, i, outs):
        return from_[i - 1, 0:outs] + from_[i, outs:2 * outs] + from_[i + 1, 2 * outs:3 * outs]

    for first_row in (0, 23):
        conv(wa, x3, parts, first_row, first_row + 7, 7)
        conv(wdt, cot3, cot_parts, first_row, first_row + 7, 7)

    def first(with_slope):
        def step(k):
            for s in range(2):
                pre = gathered(parts, 2 * k + 1 + s, 64)
                value, slope = _gelu_parts(pre)
                hidden[k, :, 256 * s:256 * s + 256] = (value * f_mask).astype(BF)
                if with_slope:
                    slope_a[k - 2, :, 256 * s:256 * s + 256] = slope
        return step
    _loop(0, 2, first(False), 2)
    _loop(2, 12, first(True), 5)
    _loop(12, 14, first(False), 2)
    clear(hidden, 3, 14)

    def pool_step(k):
        coarse3[k] = _taps((_dot(hidden[k], pool[...]) * 0.25).astype(BF).astype(F32))
    _loop(0, 14, pool_step, 14)

    conv(wb, coarse3, cparts, 0, 14, 7)

    def second(k):
        value, slope = _gelu_parts(gathered(cparts, k + 1, 128))
        middle3[k] = _taps(value * c_mask)
        slope_b[k] = slope
    _loop(0, 12, second, 6)
    clear(middle3, 2, 12)

    def third(k):
        cparts[k, 0:192] = _dot(wc[...], middle3[k])
    _loop(0, 12, third, 12)

    def third_sum(k):
        coarse_out[k] = (gathered(cparts, k + 1, 64) * c_mask).astype(BF)
    _loop(0, 10, third_sum, 10)
    clear(coarse_out, 1, 10)

    def spread_step(source):
        def step(k):
            up[k] = _dot(source[k], spread[...])
        return step
    _loop(0, 10, spread_step(coarse_out), 10)

    def join(k, s):
        both = hidden[k + 2, :, 256 * s:256 * s + 256].astype(F32) + up[k]
        joined3[2 * k - 1 + s] = _taps(both)[:, 0:128]
    join(0, 1)

    def join_step(k):
        join(k, 0)
        join(k, 1)
    _loop(1, 9, join_step, 4)
    join(9, 0)

    def out_parts(weights, source):
        def step(i):
            parts[i, :, 0:128] = _dot(weights[...], source[i])
        _loop(0, 18, step, 9)

    def out_rows(ref):
        for h in range(16):
            flat[pl.ds(h, 64, stride=16), :] = gathered(
                parts.at[:, :, pl.ds(0, 128)], h + 1, 64)
        ref[...] = flat[...].reshape(64, 16, 128).astype(BF)


    def stacked(pad, j):
        return jnp.concatenate([pad[j + 2], pad[j + 1], pad[j]], axis=0)

    def pair(one, j):
        return jnp.concatenate([one(2 * j), one(2 * j + 1)], axis=1)

    def framed(pad, first, count, own):
        pad[pl.ds(0, 2)] = jnp.zeros((2,) + pad.shape[1:], BF)
        pad[pl.ds(count + 2, 2)] = jnp.zeros((2,) + pad.shape[1:], BF)

        def step(h):
            pad[h + 2] = own(h + first)
        _loop(0, count, step, 8)

    def fine_weight_grad(pad, window, src, first):
        acc[0:192, 0:192] = jnp.zeros((192, 192), F32)

        def step(j):
            acc[0:192, 0:192] += _dot_t(pair(lambda i: stacked(pad, i), j), pair(window, j))
        _loop(0, 9, step, 9)

        def tap(t):
            if t > 8:
                return jnp.zeros((64, 64), F32)
            a, b = t // 3, t % 3
            return acc[64 * a:64 * a + 64, 64 * b:64 * b + 64]
        for t in range(5):
            both = jnp.concatenate([tap(t), tap(t + 5)], axis=1)
            src[pl.ds(first + 4 * t, 4)] = both.reshape(4, 16, 128)

    framed(pad_d, 7, 16, lambda h: cot3[h, 64:128, 0:128])
    fine_weight_grad(pad_d, lambda i: joined3[i], early_src, 36)


    def back_first(k):
        for s in range(2):
            grad = gathered(cot_parts, 2 * k + 1 + s, 64) * f_mask
            grad_joined[k, :, 256 * s:256 * s + 256] = grad.astype(BF)
    _loop(0, 14, back_first, 7)
    clear(grad_joined, 3, 14)

    def back_pool(k):
        grad_coarse3[k] = _taps(_dot(grad_joined[k], pool[...]).astype(BF).astype(F32))
    _loop(0, 14, back_pool, 14)

    framed(pad_c, 3, 8, lambda k: (grad_coarse3[k, 64:128, :].astype(F32) * own_c).astype(BF))
    acc[0:192, 0:384] = jnp.zeros((192, 384), F32)

    def c_step(j):
        acc[0:192, 0:384] += _dot_t(
            pair(lambda i: stacked(pad_c, i), j), pair(lambda i: middle3[i + 1], j))
    _loop(0, 5, c_step, 5)
    for a in range(3):
        for b in range(3):
            early_src[pl.ds(4 * (3 * a + b), 4)] = acc[
                64 * a:64 * a + 64, 128 * b:128 * b + 128].reshape(4, 16, 128)
    conv(wct, grad_coarse3, cparts, 0, 14, 7)

    def back_second(k):
        grad_b3[k] = _taps(slope_b[k] * gathered(cparts, k + 1, 128) * c_mask)
    _loop(0, 12, back_second, 6)
    clear(grad_b3, 2, 12)

    def b_own(k):
        pad_b[k] = (grad_b3[k + 2, 128:256, :].astype(F32) * own_c).astype(BF)
    _loop(0, 8, b_own, 4)

    def b_window(k):
        return jnp.concatenate([coarse3[k + 2], coarse3[k + 3], coarse3[k + 4]], axis=0)
    early_src[pl.ds(56, 36)] = jnp.zeros((36, 16, 128), F32)
    early_src[pl.ds(92, 4)] = jnp.zeros((4, 16, 128), F32)

    def b_step(j):
        early_src[pl.ds(56, 36)] += _dot_t(
            pair(b_window, j), pair(lambda k: pad_b[k], j)).reshape(36, 16, 128)
    _loop(0, 4, b_step, 4)
    early.pair()

    def back_third(k):
        cparts[k, 0:192] = _dot(wbt[...], grad_b3[k])
    _loop(0, 12, back_third, 12)

    def back_third_sum(k):
        grad_pool[k] = gathered(cparts, k + 1, 64).astype(BF)
    _loop(0, 10, back_third_sum, 10)
    _loop(0, 10, spread_step(grad_pool), 10)

    def back_join(k, s):
        at = slice(256 * s, 256 * s + 256)
        grad = grad_joined[k + 2, :, at].astype(F32) + 0.25 * up[k]
        grad_a3[2 * k - 1 + s] = _taps(slope_a[k, :, at] * grad * f_mask)[:, 0:128]
    back_join(0, 1)

    def back_join_step(k):
        back_join(k, 0)
        back_join(k, 1)
    _loop(1, 9, back_join_step, 4)
    back_join(9, 0)
    clear(grad_a3, 1, 18)
    early.plane()
    framed(pad_a, 1, 16, lambda h: grad_a3[h, 64:128, :])
    late_src[pl.ds(20, 12)] = jnp.zeros((12, 16, 128), F32)
    fine_weight_grad(pad_a, lambda i: x3[i + 6, :, 0:128], late_src, 0)
    stores = []

    def store(src, dst):
        stores.append(pltpu.make_async_copy(src, dst, store_sem.at[len(stores)]))
        stores[-1].start()

    late.pair()
    out_parts(wd, joined3)
    late.plane()
    early.along_near()
    out_rows(result_ref)
    store(result_ref, result_out)
    late.along_near()
    out_parts(wat, grad_a3)
    early.along_far()
    late.along_far()
    out_rows(input_grad_ref)
    store(input_grad_ref, input_grad_out)
    early.back_plane()
    late.back_plane()
    early.back_pair()
    late.back_pair()
    early.finish()
    store(early.whole, early_out)
    late.finish()
    store(late.whole, late_out)
    for copy in rim:
        copy.wait_send()
    for copy in stores:
        copy.wait()


def _sum_scratch(tiles):
    half, chunk = tiles // 2, tiles // 32
    buffers = [
        ((tiles, 16, 128), BF), ((tiles, 16, 128), F32),
        ((half, 16, 128), BF), ((half, 16, 128), BF), ((half, 16, 128), BF),
        ((16, chunk, 16, 128), BF), ((4, chunk, 16, 128), F32), ((4, chunk, 16, 128), F32),
    ]
    sems = [pltpu.SemaphoreType.DMA((count,)) for count in (4, 4, 16, 16, 4, 4, 4, 4, 16, 16, 4, 4)]
    return [pltpu.VMEM(shape, dtype) for shape, dtype in buffers] + sems


def levels(level_input, cotangent, ka, kb, kc, kd):
    scratch = [
        ((64, 16, 128), BF), ((64, 16, 128), BF), ((64, 16, 128), BF), ((64, 16, 128), BF),
        ((9, 64, 64), BF), ((9, 64, 128), BF), ((9, 64, 128), BF), ((9, 64, 64), BF),
        ((16, 128, 128), BF), ((128, 128), BF), ((128, 128), BF),
        ((REACH, 128, 128), BF), ((REACH, 128, 128), BF), ((128, 128), BF), ((128, 128), BF),
        ((128, 128), BF), ((128, 128), BF), ((128, 128), BF), ((128, 128), BF),
        ((192, 192), BF), ((192, 192), BF), ((384, 192), BF), ((192, 384), BF),
        ((192, 384), BF), ((384, 192), BF), ((192, 192), BF), ((192, 192), BF),
        ((512, 128), BF), ((128, 256), BF),
        ((30, 192, 256), BF), ((30, 192, 256), BF), ((30, 192, 256), F32), ((30, 192, 256), F32),
        ((14, 384, 128), F32),
        ((14, 64, 512), BF), ((10, 64, 512), F32), ((12, 128, 128), F32),
        ((14, 192, 128), BF), ((12, 384, 128), BF), ((10, 64, 128), BF),
        ((18, 192, 128), BF), ((14, 64, 512), BF), ((14, 192, 128), BF), ((12, 384, 128), BF),
        ((10, 64, 128), BF), ((10, 64, 256), F32), ((18, 192, 128), BF),
        ((20, 64, 128), BF), ((8, 128, 128), BF), ((12, 64, 128), BF), ((20, 64, 128), BF),
        ((1024, 128), F32), ((192, 512), F32),
    ]
    dma = pltpu.SemaphoreType.DMA
    out = lambda shape, dtype: jax.ShapeDtypeStruct(shape, dtype)
    return pl.pallas_call(
        _levels_kernel,
        out_shape=(
            out((64, 16, 128), BF), out((64, 16, 128), BF), out((96, 16, 128), BF), out((32, 16, 128), BF)),
        in_specs=[pl.BlockSpec(memory_space=pltpu.HBM)] * 6,
        out_specs=(pl.BlockSpec(memory_space=pltpu.HBM),) * 4,
        scratch_shapes=[pltpu.VMEM(shape, dtype) for shape, dtype in scratch]
        + [dma((6,)), dma((4,)), dma((6,)), dma((6,))] + _sum_scratch(96) + _sum_scratch(32),
        compiler_params=pltpu.CompilerParams(
            collective_id=0, has_side_effects=True, vmem_limit_bytes=60 * 1024 * 1024),
        cost_estimate=pl.CostEstimate(flops=2000000000, bytes_accessed=8000000, transcendentals=1000000),
    )(level_input, cotangent, ka, kb, kc, kd)


def _finish_kernel(fine_scale, coarse_scale, result_in, input_grad_in, early_ref, late_ref,
                   result_ref, input_grad_ref, grad_a_ref, grad_b_ref, grad_c_ref, grad_d_ref):
    result_ref[...] = result_in[...]
    input_grad_ref[...] = input_grad_in[...]
    grad_c_ref[...] = early_ref[pl.ds(0, 36)].astype(F32).reshape(9, 64, 128) * coarse_scale
    grad_b_ref[...] = early_ref[pl.ds(56, 36)].astype(F32).reshape(9, 64, 128) * coarse_scale
    for ref, taps in ((grad_d_ref, early_ref[pl.ds(36, 20)]), (grad_a_ref, late_ref[pl.ds(0, 20)])):
        fine = taps.astype(F32).reshape(5, 64, 128) * fine_scale
        ref[pl.ds(0, 5)] = fine[:, :, 0:64]
        ref[pl.ds(5, 4)] = fine[0:4, :, 64:128]


def finish(result, input_grad, early, late, fine_scale, coarse_scale):
    out = lambda shape, dtype: jax.ShapeDtypeStruct(shape, dtype)
    return pl.pallas_call(
        functools.partial(_finish_kernel, fine_scale, coarse_scale),
        out_shape=(
            out((64, 16, 128), BF), out((64, 16, 128), BF), out((9, 64, 64), F32),
            out((9, 64, 128), F32), out((9, 64, 128), F32), out((9, 64, 64), F32)),
        in_specs=[VMEM] * 4,
        out_specs=(VMEM,) * 6,
        compiler_params=pltpu.CompilerParams(vmem_limit_bytes=60 * 1024 * 1024),
        cost_estimate=pl.CostEstimate(flops=1000000, bytes_accessed=2000000, transcendentals=0),
    )(result, input_grad, early, late)


def tap_major(kernel, order):
    taps = jnp.transpose(kernel, (2, 3) + order)
    return taps.reshape((9,) + taps.shape[2:])


def from_taps(grad, order):
    return jnp.transpose(grad.reshape((3, 3) + grad.shape[1:]), order)


def body(level_input, kernel_a, kernel_b, kernel_c, kernel_d, cotangent):
    total_cells = (
        level_input.shape[1] * level_input.shape[2] * lax.axis_size("rows") * lax.axis_size("cols")
    )
    parts = levels(
        level_input, cotangent,
        tap_major(kernel_a, (0, 1)), tap_major(kernel_b, (1, 0)),
        tap_major(kernel_c, (0, 1)), tap_major(kernel_d, (0, 1)))
    result_field, input_grad, grad_a, grad_b, grad_c, grad_d = finish(
        *parts, 1.0 / math.sqrt(total_cells), 1.0 / math.sqrt(total_cells // 4))
    return (
        result_field,
        input_grad,
        from_taps(grad_a, (2, 3, 0, 1)),
        from_taps(grad_b, (3, 2, 0, 1)),
        from_taps(grad_c, (2, 3, 0, 1)),
        from_taps(grad_d, (2, 3, 0, 1)),
    )


def solution(mesh):
    placed = (P(None, "rows", "cols"), P(), P(), P(), P(), P(None, "rows", "cols"))
    return jax.shard_map(
        body,
        mesh=mesh,
        in_specs=placed,
        out_specs=(P(None, "rows", "cols"), P(None, "rows", "cols"), P(), P(), P(), P()),
        check_vma=False,
    )
```
